256 devices in a mesh: lat: 16 (over z, x_lo), lon: 16 (over y, x_hi, core).
Axes of the slice: x: 4 (x_hi: 2, x_lo: 2; x = x_hi * 2 + x_lo), y: 4, z: 8, core: 2. Of those that a mesh axis runs over, the one named last changes fastest.
Arguments:
- fine_tokens: bfloat16 [192, 384, 512], P('lat', 'lon'), may hold values from -6 to 6
- region_labels: int32 [192, 384], P('lat', 'lon'), may hold values from 0 to 5, as said below
- fine_attention_gain: float32 [512], replicated, may hold values from 0.5 to 1.5
- fine_triple_weight: bfloat16 [512, 1536], replicated, may hold values from -0.25 to 0.25
- fine_output_weight: bfloat16 [512, 512], replicated, may hold values from -0.25 to 0.25
- fine_hidden_gain: float32 [512], replicated, may hold values from 0.5 to 1.5
- fine_up_weight: bfloat16 [512, 2048], replicated, may hold values from -0.25 to 0.25
- fine_down_weight: bfloat16 [2048, 512], replicated, may hold values from -0.125 to 0.125
- merge_gain: float32 [2048], replicated, may hold values from 0.5 to 1.5
- merge_weight: bfloat16 [2048, 1024], P('lon'), may hold values from -0.125 to 0.125
- coarse_attention_gain: float32 [1024], replicated, may hold values from 0.5 to 1.5
- coarse_triple_weight: bfloat16 [1024, 3072], P(None, 'lon'), may hold values from -0.1875 to 0.1875
- coarse_output_weight: bfloat16 [1024, 1024], P('lon'), may hold values from -0.1875 to 0.1875
- coarse_hidden_gain: float32 [1024], replicated, may hold values from 0.5 to 1.5
- coarse_up_weight: bfloat16 [1024, 4096], P(None, 'lon'), may hold values from -0.1875 to 0.1875
- coarse_down_weight: bfloat16 [4096, 1024], P('lon'), may hold values from -0.09375 to 0.09375
- skip_cotangent: bfloat16 [192, 384, 512], P('lat', 'lon'), may hold values from -6 to 6
- coarse_cotangent: bfloat16 [96, 192, 1024], P('lat', 'lon'), may hold values from -6 to 6
Outputs:
- skip_tokens: bfloat16 [192, 384, 512], P('lat', 'lon')
- coarse_tokens: bfloat16 [96, 192, 1024], P('lat', 'lon')
- token_gradient: bfloat16 [192, 384, 512], P('lat', 'lon')
The draws below stay inside these ranges and needn't reach their ends.
Inputs may be any that keep to these rules, and one draw needn't show every extreme that they name: `region_labels`: tokens attend only within their window to tokens of the same label. The last 3 rows of the shifted grid carry label 1, all other rows label 0.
All inputs are finite; a program needn't handle non-finite values.
Results may differ from the reference program's by a relative error of at most 0.025.
Values may be sent and summed in bfloat16 or wider, within the bound.
A program may use at most 128 MiB of HBM per device.

```python
import jax
import jax.numpy as jnp
from jax import lax

D1 = 512
FF1 = 2048
HEADS1 = 8
D2 = 1024
FF2 = 4096
HEADS2 = 16
WIN_LAT = 6
WIN_LON = 12
LAT = 192
LON = 384
N_LON = 16


def draw_region_labels(key, part):
    key = jax.random.fold_in(key, 7)
    base_labels = jax.random.randint(key, (LAT, LON), 0, 3, dtype=jnp.int32)
    row_index = jnp.arange(LAT, dtype=jnp.int32)[:, None]
    wrapped = (row_index >= LAT - WIN_LAT // 2).astype(jnp.int32)
    return base_labels + 3 * wrapped


def block_scale(rng, shape, cuts, smallest, high):
    loudness = 1.0
    for axis_at, shards_of in cuts:
        heights = jax.random.uniform(jax.random.fold_in(jax.random.fold_in(rng, 6), axis_at), (shards_of,), jnp.float32, smallest / len(cuts), high / len(cuts))
        loudness = loudness * jnp.repeat(jnp.exp(heights), shape[axis_at] // shards_of).reshape((-1,) + (1,) * (len(shape) - 1 - axis_at))
    return loudness


def gaussian(stream_key, dims, scale, limit, shards=(), held_as=jnp.bfloat16):
    values = scale * jax.random.normal(stream_key, dims, jnp.float32)
    if shards:
        values = values * block_scale(stream_key, dims, shards, -0.22, 0.18)
    return jnp.clip(values, -limit, limit).astype(held_as)


def setup_inputs(seed: int = 0) -> dict:
    arg_keys = jax.random.split(jax.random.key(seed), 19)
    return {
        "fine_tokens": gaussian(arg_keys[0], (LAT, LON, D1), 1.0, 6.0, ((0, 16), (1, 16))),
        "region_labels": draw_region_labels(jax.random.fold_in(arg_keys[18], 71), 0),
        "fine_attention_gain": jnp.clip(1.0 + 0.1 * jax.random.normal(arg_keys[2], (D1,), jnp.float32), 0.5, 1.5),
        "fine_triple_weight": gaussian(arg_keys[3], (D1, 3 * D1), D1 ** -0.5, 0.25),
        "fine_output_weight": gaussian(arg_keys[4], (D1, D1), D1 ** -0.5, 0.25),
        "fine_hidden_gain": jnp.clip(1.0 + 0.1 * jax.random.normal(arg_keys[5], (D1,), jnp.float32), 0.5, 1.5),
        "fine_up_weight": gaussian(arg_keys[6], (D1, FF1), D1 ** -0.5, 0.25),
        "fine_down_weight": gaussian(arg_keys[7], (FF1, D1), FF1 ** -0.5, 0.125),
        "merge_gain": jnp.clip(1.0 + 0.1 * jax.random.normal(arg_keys[8], (4 * D1,), jnp.float32), 0.5, 1.5),
        "merge_weight": gaussian(arg_keys[9], (4 * D1, D2), (4 * D1) ** -0.5, 0.125, ((0, 16),)),
        "coarse_attention_gain": jnp.clip(1.0 + 0.1 * jax.random.normal(arg_keys[10], (D2,), jnp.float32), 0.5, 1.5),
        "coarse_triple_weight": gaussian(arg_keys[11], (D2, 3 * D2), D2 ** -0.5, 0.1875, ((1, 16),)),
        "coarse_output_weight": gaussian(arg_keys[12], (D2, D2), D2 ** -0.5, 0.1875, ((0, 16),)),
        "coarse_hidden_gain": jnp.clip(1.0 + 0.1 * jax.random.normal(arg_keys[13], (D2,), jnp.float32), 0.5, 1.5),
        "coarse_up_weight": gaussian(arg_keys[14], (D2, FF2), D2 ** -0.5, 0.1875, ((1, 16),)),
        "coarse_down_weight": gaussian(arg_keys[15], (FF2, D2), FF2 ** -0.5, 0.09375, ((0, 16),)),
        "skip_cotangent": gaussian(arg_keys[16], (LAT, LON, D1), 1.0, 6.0, ((0, 16), (1, 16))),
        "coarse_cotangent": gaussian(arg_keys[17], (LAT // 2, LON // 2, D2), 1.0, 6.0, ((0, 16), (1, 16))),
    }


EPSILON = 1e-05

def layer_norm(norm_input, gain_vector):
    average = lax.optimization_barrier(jnp.mean(norm_input, axis=-1, keepdims=True))
    centred = norm_input - average
    variance = lax.optimization_barrier(jnp.mean(centred * centred, axis=-1, keepdims=True))
    return centred * lax.rsqrt(variance + EPSILON) * gain_vector.astype(jnp.float32)

def to_windows(tile_field, win_rows, win_cols):
    row_count = tile_field.shape[0]
    col_count = tile_field.shape[1]
    feat_count = tile_field.shape[2]
    blocks = tile_field.reshape(row_count // win_rows, win_rows, col_count // win_cols, win_cols, feat_count)
    blocks = blocks.transpose(0, 2, 1, 3, 4)
    return blocks.reshape(row_count // win_rows * (col_count // win_cols), win_rows * win_cols, feat_count)

def from_windows(blocks, row_count, col_count, win_rows, win_cols):
    feat_count = blocks.shape[-1]
    tile_field = blocks.reshape(row_count // win_rows, col_count // win_cols, win_rows, win_cols, feat_count)
    return tile_field.transpose(0, 2, 1, 3, 4).reshape(row_count, col_count, feat_count)

def window_attention(normed, triple_weight, output_weight, labels, head_count):
    row_count, col_count, feat_width = normed.shape
    head_size = triple_weight.shape[1] // (3 * head_count)
    packed = jnp.dot(normed.reshape(row_count * col_count, feat_width), triple_weight, preferred_element_type=jnp.float32).astype(jnp.bfloat16)
    packed = to_windows(packed.reshape(row_count, col_count, 3 * head_count * head_size), WIN_LAT, WIN_LON)
    window_count = packed.shape[0]
    window_size = WIN_LAT * WIN_LON
    packed = packed.reshape(window_count, window_size, head_count, 3, head_size)
    queries = packed[:, :, :, 0].astype(jnp.float32)
    key_part = packed[:, :, :, 1].astype(jnp.float32)
    value_part = packed[:, :, :, 2].astype(jnp.float32)
    scores = jnp.einsum('wqhd,wkhd->whqk', queries, key_part) * head_size ** (-0.5)
    weights = jnp.exp(scores)
    if labels is not None:
        label_blocks = to_windows(labels.reshape(row_count, col_count, 1), WIN_LAT, WIN_LON).reshape(window_count, window_size)
        same_region = (label_blocks[:, :, None] == label_blocks[:, None, :]).astype(jnp.float32)
        weights = weights * same_region[:, None]
    attn_probs = (weights / lax.optimization_barrier(jnp.sum(weights, axis=-1, keepdims=True))).astype(jnp.bfloat16)
    mixed_heads = jnp.einsum('whqk,wkhd->wqhd', attn_probs.astype(jnp.float32), value_part).astype(jnp.bfloat16)
    mixed_heads = from_windows(mixed_heads.reshape(window_count, window_size, head_count * head_size), row_count, col_count, WIN_LAT, WIN_LON)
    projected = jnp.dot(mixed_heads.reshape(row_count * col_count, head_count * head_size), output_weight, preferred_element_type=jnp.float32)
    return projected.reshape(row_count, col_count, output_weight.shape[1])

def hidden_part(normed, up_weight, down_weight):
    feat_width = normed.shape[-1]
    lifted = jnp.dot(normed.reshape(-1, feat_width), up_weight, preferred_element_type=jnp.float32)
    active = jax.nn.gelu(lifted, approximate=False).astype(jnp.bfloat16)
    lowered = jnp.dot(active, down_weight, preferred_element_type=jnp.float32)
    return lowered.reshape(normed.shape[:-1] + (down_weight.shape[1],))

def fine_block(fine_start, labels, attention_gain, triple_weight, output_weight, hidden_gain, up_weight, down_weight):
    normed = layer_norm(fine_start, attention_gain).astype(jnp.bfloat16)
    residual = fine_start + window_attention(normed, triple_weight, output_weight, labels, HEADS1)
    normed_two = layer_norm(residual, hidden_gain).astype(jnp.bfloat16)
    return (residual + hidden_part(normed_two, up_weight, down_weight)).astype(jnp.bfloat16)

def merge_patches(skip_float, merge_gain, merge_weight):
    row_count, col_count, feat_width = skip_float.shape
    quad_blocks = skip_float.reshape(row_count // 2, 2, col_count // 2, 2, feat_width).transpose(0, 2, 3, 1, 4)
    joined = quad_blocks.reshape(row_count // 2, col_count // 2, 4 * feat_width)
    normed = layer_norm(joined, merge_gain).astype(jnp.bfloat16)
    projected = jnp.dot(normed.reshape(-1, 4 * feat_width), merge_weight, preferred_element_type=jnp.float32)
    return projected.astype(jnp.bfloat16).reshape(row_count // 2, col_count // 2, merge_weight.shape[1])

def reference(fine_tokens, region_labels, fine_attention_gain, fine_triple_weight, fine_output_weight, fine_hidden_gain, fine_up_weight, fine_down_weight, merge_gain, merge_weight, coarse_attention_gain, coarse_triple_weight, coarse_output_weight, coarse_hidden_gain, coarse_up_weight, coarse_down_weight, skip_cotangent, coarse_cotangent):
    lat_step = WIN_LAT // 2
    lon_step = WIN_LON // 2
    rolled = jnp.roll(fine_tokens, (-lat_step, -lon_step), axis=(0, 1))

    def fine_map(fine_start):
        return fine_block(fine_start, region_labels, fine_attention_gain, fine_triple_weight, fine_output_weight, fine_hidden_gain, fine_up_weight, fine_down_weight)
    rolled_out, fine_pull = jax.vjp(fine_map, rolled.astype(jnp.float32))
    skip_tokens = jnp.roll(rolled_out, (lat_step, lon_step), axis=(0, 1))

    def merge_map(skip_float):
        return merge_patches(skip_float, merge_gain, merge_weight)
    merged, merge_pull = jax.vjp(merge_map, skip_tokens.astype(jnp.float32))
    coarse_input = merged.astype(jnp.float32)

    def first_norm(norm_input):
        return layer_norm(norm_input, coarse_attention_gain)

    def second_norm(norm_input):
        return layer_norm(norm_input, coarse_hidden_gain)
    normed_first, first_pull = jax.vjp(first_norm, coarse_input)
    normed_one = normed_first.astype(jnp.bfloat16)
    group_count = N_LON
    group_heads = HEADS2 // group_count
    triple_groups = coarse_triple_weight.reshape(D2, group_count, -1).transpose(1, 0, 2)
    output_groups = coarse_output_weight.reshape(group_count, -1, D2)
    up_groups = coarse_up_weight.reshape(D2, group_count, -1).transpose(1, 0, 2)
    down_groups = coarse_down_weight.reshape(group_count, -1, D2)
    zero_field = jnp.zeros(coarse_input.shape, jnp.float32)

    def attention_step(running_sum, group_weights):
        group_term = window_attention(normed_one, group_weights[0], group_weights[1], None, group_heads)
        rounded = lax.optimization_barrier(group_term.astype(jnp.bfloat16))
        return (running_sum + rounded.astype(jnp.float32), None)
    coarse_attended = lax.scan(attention_step, zero_field, (triple_groups, output_groups))[0]
    coarse_residual = coarse_input + coarse_attended
    normed_second, second_pull = jax.vjp(second_norm, coarse_residual)
    normed_two = normed_second.astype(jnp.bfloat16)

    def hidden_step(running_sum, group_weights):
        group_term = hidden_part(normed_two, group_weights[0], group_weights[1])
        rounded = lax.optimization_barrier(group_term.astype(jnp.bfloat16))
        return (running_sum + rounded.astype(jnp.float32), None)
    coarse_hidden = lax.scan(hidden_step, zero_field, (up_groups, down_groups))[0]
    coarse_tokens = (coarse_residual + coarse_hidden).astype(jnp.bfloat16)
    cotangent_float = coarse_cotangent.astype(jnp.float32)

    def hidden_grad_step(running_sum, group_weights):

        def group_map(norm_value):
            return hidden_part(norm_value, group_weights[0], group_weights[1])
        group_pull = jax.vjp(group_map, normed_two)[1]
        return (running_sum + group_pull(cotangent_float)[0].astype(jnp.float32), None)
    grad_two = lax.scan(hidden_grad_step, zero_field, (up_groups, down_groups))[0]
    grad_residual = cotangent_float + second_pull(grad_two)[0]
    grad_round = lax.optimization_barrier(grad_residual.astype(jnp.bfloat16)).astype(jnp.float32)

    def attention_grad_step(running_sum, group_weights):

        def group_map(norm_value):
            return window_attention(norm_value, group_weights[0], group_weights[1], None, group_heads)
        group_pull = jax.vjp(group_map, normed_one)[1]
        return (running_sum + group_pull(grad_round)[0].astype(jnp.float32), None)
    grad_one = lax.scan(attention_grad_step, zero_field, (triple_groups, output_groups))[0]
    grad_merged = grad_residual + first_pull(grad_one)[0]
    grad_from_merge = merge_pull(grad_merged.astype(jnp.bfloat16))[0]
    grad_skip = (skip_cotangent.astype(jnp.float32) + grad_from_merge).astype(jnp.bfloat16)
    grad_rolled = jnp.roll(grad_skip, (-lat_step, -lon_step), axis=(0, 1))
    grad_start = fine_pull(grad_rolled)[0]
    token_gradient = jnp.roll(grad_start.astype(jnp.bfloat16), (lat_step, lon_step), axis=(0, 1))
    return (skip_tokens, coarse_tokens, token_gradient)
```

```python
import functools

import jax
import jax.numpy as jnp
import ml_dtypes
import numpy as np
from jax import lax
from jax.experimental import pallas as pl
from jax.experimental.pallas import tpu as pltpu
from jax.sharding import PartitionSpec as P

MESH = pl.DeviceIdType.MESH
F32 = jnp.float32
BF16 = jnp.bfloat16
EPSILON = 1e-05
SCALE = 0.125
ROWS, COLS = 12, 24
TOKENS = ROWS * COLS
WIN = 72
HALO = 160
PARTS = ((0, 64), (64, 64), (128, 32))


def tok_index(r, c):
    return r * COLS + c


def win_index(r, c):
    return ((r // 6) * 2 + c // 12) * WIN + (r % 6) * 12 + c % 12


def join_index(r, c):
    return (2 * (c % 2) + r % 2) * WIN + (r // 2) * 12 + c // 2


@functools.cache
def tables():
    def forward(source):
        pack = np.zeros((HALO, TOKENS), np.float32)
        own = np.zeros((TOKENS, TOKENS), np.float32)
        got = np.zeros((TOKENS, HALO), np.float32)
        for r in range(ROWS):
            for c in range(COLS):
                far_r, far_c = r + 3 >= ROWS, c + 6 >= COLS
                at = source((r + 3) % ROWS, (c + 6) % COLS)
                if not far_r and not far_c:
                    own[win_index(r, c), at] = 1
                    continue
                if far_r and not far_c:
                    slot = (r - 9) * 18 + c
                elif far_c and not far_r:
                    slot = 64 + r * 6 + (c - 18)
                else:
                    slot = 128 + (r - 9) * 6 + (c - 18)
                pack[slot, at] = 1
                got[win_index(r, c), slot] = 1
        return pack, own, got

    def back(target):
        pack = np.zeros((HALO, TOKENS), np.float32)
        own = np.zeros((TOKENS, TOKENS), np.float32)
        got = np.zeros((TOKENS, HALO), np.float32)
        for r in range(ROWS):
            for c in range(COLS):
                far_r, far_c = r < 3, c < 6
                at = win_index((r - 3) % ROWS, (c - 6) % COLS)
                if not far_r and not far_c:
                    own[target(r, c), at] = 1
                    continue
                if far_r and not far_c:
                    slot = r * 18 + (c - 6)
                elif far_c and not far_r:
                    slot = 64 + (r - 3) * 6 + c
                else:
                    slot = 128 + r * 6 + c
                pack[slot, at] = 1
                got[target(r, c), slot] = 1
        return pack, own, got

    def plain(target):
        move = np.zeros((TOKENS, TOKENS), np.float32)
        for r in range(ROWS):
            for c in range(COLS):
                move[target(r, c), tok_index(r, c)] = 1
        return move

    tok_pack, tok_own, roll_got = forward(tok_index)
    join_pack, join_own, _ = forward(join_index)
    back_pack, back_own, back_got = back(tok_index)
    _, back_own_join, back_got_join = back(join_index)
    every = (
        tok_pack, tok_own, roll_got, join_pack, join_own, back_pack, back_own, back_got,
        back_own_join, back_got_join, plain(join_index), plain(win_index),
    )
    return tuple(m.astype(ml_dtypes.bfloat16) for m in every)


def mm(a, b):
    return lax.dot_general(a, b, (((1,), (0,)), ((), ())), preferred_element_type=F32)


def mm_t(a, b):
    return lax.dot_general(a, b, (((1,), (1,)), ((), ())), preferred_element_type=F32)


def t_mm(a, b):
    return lax.dot_general(a, b, (((0,), (0,)), ((), ())), preferred_element_type=F32)


def rounded(v):
    return v.astype(BF16).astype(F32)


def standard(v):
    centred = v - jnp.mean(v, axis=-1, keepdims=True)
    scale = lax.rsqrt(jnp.mean(centred * centred, axis=-1, keepdims=True) + EPSILON)
    return centred * scale, scale


def norm_pull(grad, gain, xhat, scale):
    d = grad * gain
    return scale * (
        d - jnp.mean(d, axis=-1, keepdims=True) - xhat * jnp.mean(d * xhat, axis=-1, keepdims=True)
    )


def gelu_both(x):
    cdf = 0.5 * (1.0 + lax.erf(x * 0.7071067811865476))
    slope = cdf + x * jnp.exp(-0.5 * x * x) * 0.3989422804014327
    return x * cdf, slope


def attend(q, k, v, mask):
    e = jnp.exp(mm_t(q, k) * SCALE)
    if mask is not None:
        e = e * mask
    p = e * (1.0 / jnp.sum(e, axis=-1, keepdims=True))
    return p, mm(p.astype(BF16), v)


def attend_pull(q, k, v, p, dm):
    dv = t_mm(p.astype(BF16), dm)
    dp = rounded(mm_t(dm, v))
    ds = (p * (dp - jnp.sum(dp * p, axis=-1, keepdims=True)) * SCALE).astype(BF16)
    return mm(ds, k), t_mm(ds, q), dv


def loop(count, body):
    def step(i, carry):
        body(i)
        return carry

    lax.fori_loop(0, count, step, 0)


def chunk(i, size):
    return pl.ds(pl.multiple_of(i * size, size), size)


MERGE, TRIPLE, OUTPUT, UP, DOWN = range(5)
SLOTS = 17


class Gather:
    def __init__(self, shards, full, local_sem, send_sem, recv_sem):
        self.shards, self.full = shards, full
        self.local_sem, self.send_sem, self.recv_sem = local_sem, send_sem, recv_sem
        lat, lon = lax.axis_index("lat"), lax.axis_index("lon")
        self.z, self.xl = lat // 2, lat % 2
        self.y, self.xh, self.c = lon // 4, (lon // 2) % 2, lon % 2
        self.lat, self.lon = lat, lon
        self.up = (self.y + 1) % 4
        self.dn = (self.y + 3) % 4
        self.op = (self.y + 2) % 4
        self.copies = {}

    def place(self, z, xl, y, xh, c):
        return {"lat": z * 2 + xl, "lon": y * 4 + xh * 2 + c}

    def neighbours(self):
        z, xl, y, xh, c = self.z, self.xl, self.y, self.xh, self.c
        return [
            self.place(z, 1 - xl, y, 1 - xh, c),
            self.place(z, xl, self.up, xh, c),
            self.place(z, xl, self.dn, xh, c),
            self.place((z + 1) % 8, xl, y, xh, c),
            self.place((z + 7) % 8, xl, y, xh, c),
            self.place(z, xl, y, xh, 1 - c),
        ]

    def half(self, a):
        size = self.shards[a].shape[0] // 2
        return pl.ds(pl.multiple_of((self.z % 2) * size, size), size)

    def send(self, a, slot, src, dst, who):
        copy = pltpu.make_async_remote_copy(
            src_ref=src,
            dst_ref=dst,
            send_sem=self.send_sem.at[a, slot],
            recv_sem=self.recv_sem.at[a, slot],
            device_id=self.neighbours()[who],
            device_id_type=MESH,
        )
        copy.start()
        self.copies[a, slot] = copy

    def got(self, a, slot):
        self.copies[a, slot].wait_recv()

    def tick(self, step, a):
        shard, full, half = self.shards[a], self.full[a], self.half(a)
        y, xh, c, up, dn, op = self.y, self.xh, self.c, self.up, self.dn, self.op
        if step == 0:
            self.send(a, 0, shard, full.at[y, xh, c], 0)
            self.send(a, 1, shard.at[half], full.at[y, xh, c, half], 1)
            self.send(a, 2, shard.at[half], full.at[y, xh, c, half], 2)
            self.local = getattr(self, "local", {})
            self.local[a] = pltpu.make_async_copy(shard, full.at[y, xh, c], self.local_sem.at[a])
            self.local[a].start()
        elif step == 1:
            self.got(a, 0)
            other = full.at[y, 1 - xh, c, half]
            self.send(a, 3, other, other, 1)
            self.send(a, 4, other, other, 2)
            self.local[a].wait()
            self.send(a, 13, full.at[y, :, c], full.at[y, :, c], 5)
        elif step == 2:
            for slot, far, pick, who in ((5, dn, 0, 1), (6, up, 1, 2)):
                self.got(a, slot - 4)
                self.got(a, slot - 2)
                piece = full.at[far, pick, c, half]
                self.send(a, slot, piece, piece, who)
                base = 7 + 2 * (slot - 5)
                for d in (0, 1):
                    piece = full.at[far, d, c, half]
                    self.send(a, base + d, piece, piece, 3 + d)
        elif step == 3:
            for d in (0, 1):
                self.got(a, 5 + d)
                piece = full.at[op, d, c, half]
                self.send(a, 11 + d, piece, piece, 3 + d)
        elif step == 4:
            for i, far in enumerate((dn, up, op)):
                self.got(a, 7 + 2 * i)
                self.got(a, 8 + 2 * i)
                piece = full.at[far, :, c]
                self.send(a, 14 + i, piece, piece, 5)
        else:
            for i in range(4):
                self.got(a, 13 + i)

    def finish(self):
        for copy in self.copies.values():
            copy.wait_send()


POINTS = {
    "start": [(0, a) for a in range(5)],
    "qkv": [(1, MERGE)],
    "attention": [(2, MERGE), (1, TRIPLE)],
    "proj": [(3, MERGE), (1, OUTPUT)],
    "up": [(4, MERGE), (2, TRIPLE), (2, OUTPUT)],
    "down": [(1, UP), (3, TRIPLE), (3, OUTPUT)],
    "merge": [(5, MERGE)],
    "coarse": [(2, UP), (1, DOWN), (4, TRIPLE), (4, OUTPUT), (5, TRIPLE)],
    "coarse_out": [(3, UP), (2, DOWN), (5, OUTPUT)],
    "hidden": [(4, UP), (3, DOWN), (4, DOWN), (5, UP), (5, DOWN)],
}


def kernel(*refs):
    (
        tok, onehot, g1, wt, wo, g2, wu, wd, gm, s_merge, cg1, s_triple, s_output, cg2, s_up, s_down,
        skip_cot, coarse_cot,
        m_tok_pack, m_tok_own, m_roll_got, m_join_pack, m_join_own, m_back_pack, m_back_own, m_back_got,
        m_back_own_join, m_back_got_join, m_tok_join, m_tok_win,
        skip_out, coarse_out, grad_out,
        f_merge, f_triple, f_output, f_up, f_down,
        x_ref, n_ref, lab_ref, qkv_ref, p_ref, mix_ref, res_ref, act_ref, slope_ref, win_ref,
        grad_ref, dres_ref, dqkv_ref,
        j_ref, nj_ref, mg_ref, cn_ref, cqkv_ref, cp_ref, cmix_ref, cres_ref, cot_ref, hid_ref, dn_ref, cdqkv_ref,
        halo_send, halo_recv, local_sem, send_sem, recv_sem, halo_ssem, halo_rsem,
    ) = refs
    gather = Gather(
        (s_merge, s_triple, s_output, s_up, s_down), (f_merge, f_triple, f_output, f_up, f_down),
        local_sem, send_sem, recv_sem,
    )
    lat, lon = gather.lat, gather.lon
    north, south, west, east = (lat + 15) % 16, (lat + 1) % 16, (lon + 15) % 16, (lon + 1) % 16
    ahead = [{"lat": north, "lon": lon}, {"lat": lat, "lon": west}, {"lat": north, "lon": west}]
    behind = [{"lat": south, "lon": lon}, {"lat": lat, "lon": east}, {"lat": south, "lon": east}]
    everyone = gather.neighbours() + ahead + behind

    barrier = pltpu.get_barrier_semaphore()
    for who in everyone:
        pl.semaphore_signal(barrier, inc=1, device_id=who, device_id_type=MESH)
    pl.semaphore_wait(barrier, len(everyone))

    def point(name):
        for step, a in POINTS[name]:
            gather.tick(step, a)

    def exchange(k, value, targets):
        halo_send[k] = value.astype(BF16)
        copies = []
        for i, (first, size) in enumerate(PARTS):
            rows = pl.ds(first, size)
            copy = pltpu.make_async_remote_copy(
                src_ref=halo_send.at[k, rows],
                dst_ref=halo_recv.at[k, rows],
                send_sem=halo_ssem.at[k, i],
                recv_sem=halo_rsem.at[k, i],
                device_id=targets[i],
                device_id_type=MESH,
            )
            copy.start()
            copies.append(copy)
        return copies

    def settle(copies):
        for copy in copies:
            copy.wait()

    copies = exchange(0, mm(m_tok_pack[...], tok[...]), ahead)
    point("start")
    lab_ref[...] = mm(m_tok_win[...], onehot[...])
    x_ref[...] = mm(m_tok_own[...], tok[...])
    settle(copies)
    x_ref[...] += mm(m_roll_got[...], halo_recv[0])

    def first_norm(i):
        rows = chunk(i, 96)
        n_ref[rows] = (standard(x_ref[rows])[0] * g1[...]).astype(BF16)

    loop(3, first_norm)

    def project(i):
        cols = chunk(i, 256)
        qkv_ref[:, cols] = rounded(mm(n_ref[...], wt[:, cols]))

    loop(6, project)
    point("qkv")

    def fine_attention(w):
        rows = chunk(w, WIN)
        seen = lab_ref[rows].astype(BF16)
        mask = mm_t(seen, seen)
        for pair in range(4):
            mixed = []
            for h in (2 * pair, 2 * pair + 1):
                q, k, v = (
                    qkv_ref[rows, h * 192 + 64 * i : h * 192 + 64 * i + 64].astype(BF16) for i in range(3)
                )
                p, m = attend(q, k, v, mask)
                p_ref[w * 8 + h] = p
                mixed.append(m)
            mix_ref[rows, pair * 128 : pair * 128 + 128] = jnp.concatenate(mixed, axis=-1)

    loop(4, fine_attention)
    point("attention")

    def out_project(i):
        cols = chunk(i, 256)
        res_ref[:, cols] = x_ref[:, cols] + mm(mix_ref[...].astype(BF16), wo[:, cols])

    loop(2, out_project)

    def second_norm(i):
        rows = chunk(i, 96)
        n_ref[rows] = (standard(res_ref[rows])[0] * g2[...]).astype(BF16)

    loop(3, second_norm)
    point("proj")

    def lift(i):
        cols = chunk(i, 256)
        active, slope = gelu_both(mm(n_ref[...], wu[:, cols]))
        act_ref[:, cols] = active.astype(BF16)
        slope_ref[:, cols] = slope.astype(BF16)

    loop(8, lift)
    point("up")

    def lower(i):
        cols = chunk(i, 256)
        win_ref[:, cols] = (res_ref[:, cols] + mm(act_ref[...], wd[:, cols])).astype(BF16)

    loop(2, lower)
    copies = exchange(1, mm(m_back_pack[...], win_ref[...]), behind)
    point("down")
    j_ref[...] = mm(m_back_own_join[...], win_ref[...])
    x_kept = mm(m_back_own[...], win_ref[...])
    settle(copies)
    j_ref[...] += mm(m_back_got_join[...], halo_recv[1])
    skip_out[...] = (x_kept + mm(m_back_got[...], halo_recv[1])).astype(BF16)

    quads = [pl.ds(q * WIN, WIN) for q in range(4)]

    def joined_standard():
        average = sum(jnp.sum(j_ref[q], axis=-1, keepdims=True) for q in quads) * (1.0 / 2048)
        square = 0.0
        for q in quads:
            centred = j_ref[q] - average
            square = square + jnp.sum(centred * centred, axis=-1, keepdims=True)
        return average, lax.rsqrt(square * (1.0 / 2048) + EPSILON)

    average, merge_scale = joined_standard()
    for i, q in enumerate(quads):
        nj_ref[:, i * 512 : i * 512 + 512] = (
            (j_ref[q] - average) * merge_scale * gm[:, i * 512 : i * 512 + 512]
        ).astype(BF16)
    for i in range(6):
        cot_ref[i * 12 : i * 12 + 12] = coarse_cot[i].astype(F32)
    point("merge")

    def merge(i):
        cols = chunk(i, 256)
        weight = f_merge[:, :, :, :, cols].reshape(2048, 256)
        mg_ref[:, cols] = rounded(mm(nj_ref[...], weight))

    loop(4, merge)

    xhat, scale = standard(mg_ref[...])
    cn_ref[...] = (xhat * cg1[...]).astype(BF16)
    point("coarse")

    def coarse_attention(y):
        mixed = []
        for i in range(4):
            part = mm(cn_ref[...], f_triple[y, i // 2, i % 2]).astype(BF16)
            cqkv_ref[y * 4 + i] = part.astype(F32)
            p, m = attend(part[:, :64], part[:, 64:128], part[:, 128:], None)
            cp_ref[y * 4 + i] = p
            mixed.append(m)
        cmix_ref[:, chunk(y, 256)] = jnp.concatenate(mixed, axis=-1).astype(BF16)

    loop(4, coarse_attention)
    point("coarse_out")

    def coarse_project(i):
        cols = chunk(i, 256)
        weight = f_output[:, :, :, :, cols].reshape(1024, 256)
        cres_ref[:, cols] = mg_ref[:, cols] + mm(cmix_ref[...], weight)

    loop(4, coarse_project)
    xhat, scale = standard(cres_ref[...])
    cn_ref[...] = (xhat * cg2[...]).astype(BF16)
    hid_ref[...] = cres_ref[...]
    dn_ref[...] = jnp.zeros_like(dn_ref)
    point("hidden")

    def coarse_hidden(y):
        for i in range(4):
            upper, lower_weight = f_up[y, i // 2, i % 2], f_down[y, i // 2, i % 2]
            active, slope = gelu_both(mm(cn_ref[...], upper))
            hid_ref[...] += mm(active.astype(BF16), lower_weight)
            grad = rounded(mm_t(cot_ref[...].astype(BF16), lower_weight))
            dn_ref[...] += mm_t((grad * slope).astype(BF16), upper)

    loop(4, coarse_hidden)
    for i in range(6):
        coarse_out[i] = hid_ref[i * 12 : i * 12 + 12].astype(BF16)
    xhat, scale = standard(cres_ref[...])
    cres_ref[...] = cot_ref[...] + norm_pull(dn_ref[...], cg2[...], xhat, scale)

    def coarse_mix_pull(i):
        rows_of = f_output[i].reshape(256, 1024)
        cmix_ref[:, chunk(i, 256)] = mm_t(cres_ref[...].astype(BF16), rows_of).astype(BF16)

    loop(4, coarse_mix_pull)
    dn_ref[...] = jnp.zeros_like(dn_ref)

    def coarse_attention_pull(y):
        dmix = cmix_ref[:, chunk(y, 256)]
        for i in range(4):
            part = cqkv_ref[y * 4 + i].astype(BF16)
            dq, dk, dv = attend_pull(
                part[:, :64], part[:, 64:128], part[:, 128:], cp_ref[y * 4 + i], dmix[:, i * 64 : i * 64 + 64]
            )
            packed = jnp.concatenate([dq, dk, dv], axis=-1).astype(BF16)
            dn_ref[...] += mm_t(packed, f_triple[y, i // 2, i % 2])

    loop(4, coarse_attention_pull)
    xhat, scale = standard(mg_ref[...])
    cn_ref[...] = (cres_ref[...] + norm_pull(dn_ref[...], cg1[...], xhat, scale)).astype(BF16)

    def merge_pull(y):
        res_rows = chunk(y, WIN)
        grad_ref[res_rows] = rounded(mm_t(cn_ref[...], f_merge[y].reshape(512, 1024)))

    loop(4, merge_pull)
    first = 0.0
    second = 0.0
    for i, q in enumerate(quads):
        d = grad_ref[q] * gm[:, i * 512 : i * 512 + 512]
        first = first + jnp.sum(d, axis=-1, keepdims=True)
        second = second + jnp.sum(d * (j_ref[q] - average), axis=-1, keepdims=True)
    first = first * (1.0 / 2048)
    second = second * merge_scale * (1.0 / 2048)
    dqkv_ref[:, :512] = mm(m_tok_join[...], skip_cot[...])
    for i, q in enumerate(quads):
        d = grad_ref[q] * gm[:, i * 512 : i * 512 + 512]
        xhat = (j_ref[q] - average) * merge_scale
        grad_ref[q] = dqkv_ref[q, :512] + merge_scale * (d - first - xhat * second)

    win_ref[...] = grad_ref[...].astype(BF16)
    copies = exchange(2, mm(m_join_pack[...], win_ref[...]), ahead)
    grad_ref[...] = mm(m_join_own[...], win_ref[...])
    settle(copies)
    grad_ref[...] += mm(m_roll_got[...], halo_recv[2])

    def lower_pull(i):
        cols = chunk(i, 256)
        grad = rounded(mm_t(grad_ref[...].astype(BF16), wd[cols]))
        act_ref[:, cols] = (grad * slope_ref[:, cols].astype(F32)).astype(BF16)

    loop(8, lower_pull)

    def lift_pull(i):
        rows = chunk(i, 256)
        dres_ref[:, rows] = rounded(mm_t(act_ref[...], wu[rows]))

    loop(2, lift_pull)

    def second_pull(i):
        rows = chunk(i, 96)
        xhat, scale = standard(res_ref[rows])
        total = grad_ref[rows] + norm_pull(dres_ref[rows], g2[...], xhat, scale)
        dres_ref[rows] = total
        n_ref[rows] = total.astype(BF16)

    loop(3, second_pull)

    def out_pull(i):
        rows = chunk(i, 256)
        mix_ref[:, rows] = rounded(mm_t(n_ref[...], wo[rows]))

    loop(2, out_pull)

    def fine_attention_pull(w):
        rows = chunk(w, WIN)
        for pair in range(4):
            packed = []
            for h in (2 * pair, 2 * pair + 1):
                q, k, v = (
                    qkv_ref[rows, h * 192 + 64 * i : h * 192 + 64 * i + 64].astype(BF16) for i in range(3)
                )
                dm = mix_ref[rows, h * 64 : h * 64 + 64].astype(BF16)
                packed.extend(attend_pull(q, k, v, p_ref[w * 8 + h], dm))
            dqkv_ref[rows, pair * 384 : pair * 384 + 384] = jnp.concatenate(packed, axis=-1)

    loop(4, fine_attention_pull)

    def project_pull(i):
        rows = chunk(i, 256)
        grad_ref[:, rows] = rounded(mm_t(dqkv_ref[...].astype(BF16), wt[rows]))

    loop(2, project_pull)

    def first_pull(i):
        rows = chunk(i, 96)
        xhat, scale = standard(x_ref[rows])
        win_ref[rows] = (dres_ref[rows] + norm_pull(grad_ref[rows], g1[...], xhat, scale)).astype(BF16)

    loop(3, first_pull)
    copies = exchange(3, mm(m_back_pack[...], win_ref[...]), behind)
    grad_ref[...] = mm(m_back_own[...], win_ref[...])
    gather.finish()
    settle(copies)
    grad_out[...] = (grad_ref[...] + mm(m_back_got[...], halo_recv[3])).astype(BF16)


def local(
    fine_tokens, region_labels, g1, wt, wo, g2, wu, wd, gm, s_merge, cg1, s_triple, s_output, cg2, s_up, s_down,
    skip_cot, coarse_cot,
):
    onehot = (region_labels.reshape(TOKENS, 1) == jnp.arange(128, dtype=jnp.int32)[None]).astype(BF16)
    moves = [jnp.asarray(m) for m in tables()]
    vmem = pl.BlockSpec(memory_space=pltpu.VMEM)
    held = pl.BlockSpec(memory_space=pl.ANY)
    shards = (s_merge, s_triple, s_output, s_up, s_down)
    args = [
        fine_tokens.reshape(TOKENS, 512), onehot, g1[None], wt, wo, g2[None], wu, wd, gm[None], s_merge, cg1[None],
        s_triple, s_output, cg2[None], s_up, s_down, skip_cot.reshape(TOKENS, 512), coarse_cot, *moves,
    ]
    in_specs = [held if any(a is s for s in shards) else vmem for a in args]
    f32 = lambda *shape: pltpu.VMEM(shape, F32)
    bf16 = lambda *shape: pltpu.VMEM(shape, BF16)
    scratch = [bf16(4, 2, 2, *s.shape) for s in shards]
    scratch += [
        f32(288, 512), bf16(288, 512), f32(288, 128), f32(288, 1536), f32(32, 72, 72), f32(288, 512),
        f32(288, 512), bf16(288, 2048), bf16(288, 2048), bf16(288, 512),
        f32(288, 512), f32(288, 512), f32(288, 1536),
        f32(288, 512), bf16(72, 2048), f32(72, 1024), bf16(72, 1024), f32(16, 72, 192), f32(16, 72, 72),
        bf16(72, 1024), f32(72, 1024), f32(72, 1024), f32(72, 1024), f32(72, 1024), f32(8, 128),
        bf16(4, HALO, 512), bf16(4, HALO, 512),
        pltpu.SemaphoreType.DMA((5,)), pltpu.SemaphoreType.DMA((5, SLOTS)), pltpu.SemaphoreType.DMA((5, SLOTS)),
        pltpu.SemaphoreType.DMA((4, 3)), pltpu.SemaphoreType.DMA((4, 3)),
    ]
    skip, coarse, grad = pl.pallas_call(
        kernel,
        out_shape=[
            jax.ShapeDtypeStruct((TOKENS, 512), BF16),
            jax.ShapeDtypeStruct((6, 12, 1024), BF16),
            jax.ShapeDtypeStruct((TOKENS, 512), BF16),
        ],
        in_specs=in_specs,
        out_specs=[vmem] * 3,
        scratch_shapes=scratch,
        compiler_params=pltpu.CompilerParams(
            collective_id=0, has_side_effects=True, vmem_limit_bytes=60 * 1024 * 1024
        ),
        name="backbone",
    )(*args)
    return skip.reshape(ROWS, COLS, 512), coarse, grad.reshape(ROWS, COLS, 512)


def solution(mesh):
    in_specs = (
        P("lat", "lon", None), P("lat", "lon"), P(), P(), P(), P(), P(), P(), P(), P("lon", None), P(),
        P(None, "lon"), P("lon", None), P(), P(None, "lon"), P("lon", None),
        P("lat", "lon", None), P("lat", "lon", None),
    )
    out_specs = (P("lat", "lon", None), P("lat", "lon", None), P("lat", "lon", None))
    return jax.shard_map(local, mesh=mesh, in_specs=in_specs, out_specs=out_specs, check_vma=False)
```

```python
import functools

import jax
import jax.numpy as jnp
import ml_dtypes
import numpy as np
from jax import lax
from jax.experimental import pallas as pl
from jax.experimental.pallas import tpu as pltpu
from jax.sharding import PartitionSpec as P

MESH = pl.DeviceIdType.MESH
F32 = jnp.float32
BF16 = jnp.bfloat16
EPSILON = 1e-05
SCALE = 0.125
ROWS, COLS = 12, 24
TOKENS = ROWS * COLS
WIN = 72
HALO = 160
PARTS = ((0, 64), (64, 64), (128, 32))


def tok_index(r, c):
    return r * COLS + c


def win_index(r, c):
    return ((r // 6) * 2 + c // 12) * WIN + (r % 6) * 12 + c % 12


def join_index(r, c):
    return (2 * (c % 2) + r % 2) * WIN + (r // 2) * 12 + c // 2


@functools.cache
def tables():
    def forward(source):
        pack = np.zeros((HALO, TOKENS), np.float32)
        own = np.zeros((TOKENS, TOKENS), np.float32)
        got = np.zeros((TOKENS, HALO), np.float32)
        for r in range(ROWS):
            for c in range(COLS):
                far_r, far_c = r + 3 >= ROWS, c + 6 >= COLS
                at = source((r + 3) % ROWS, (c + 6) % COLS)
                if not far_r and not far_c:
                    own[win_index(r, c), at] = 1
                    continue
                if far_r and not far_c:
                    slot = (r - 9) * 18 + c
                elif far_c and not far_r:
                    slot = 64 + r * 6 + (c - 18)
                else:
                    slot = 128 + (r - 9) * 6 + (c - 18)
                pack[slot, at] = 1
                got[win_index(r, c), slot] = 1
        return pack, own, got

    def back(target):
        pack = np.zeros((HALO, TOKENS), np.float32)
        own = np.zeros((TOKENS, TOKENS), np.float32)
        got = np.zeros((TOKENS, HALO), np.float32)
        for r in range(ROWS):
            for c in range(COLS):
                far_r, far_c = r < 3, c < 6
                at = win_index((r - 3) % ROWS, (c - 6) % COLS)
                if not far_r and not far_c:
                    own[target(r, c), at] = 1
                    continue
                if far_r and not far_c:
                    slot = r * 18 + (c - 6)
                elif far_c and not far_r:
                    slot = 64 + (r - 3) * 6 + c
                else:
                    slot = 128 + r * 6 + c
                pack[slot, at] = 1
                got[target(r, c), slot] = 1
        return pack, own, got

    def plain(target):
        move = np.zeros((TOKENS, TOKENS), np.float32)
        for r in range(ROWS):
            for c in range(COLS):
                move[target(r, c), tok_index(r, c)] = 1
        return move

    tok_pack, tok_own, roll_got = forward(tok_index)
    join_pack, join_own, _ = forward(join_index)
    back_pack, back_own, back_got = back(tok_index)
    _, back_own_join, back_got_join = back(join_index)
    every = (
        tok_pack, tok_own, roll_got, join_pack, join_own, back_pack, back_own, back_got,
        back_own_join, back_got_join, plain(join_index), plain(win_index),
    )
    return tuple(m.astype(ml_dtypes.bfloat16) for m in every)


def mm(a, b):
    return lax.dot_general(a, b, (((1,), (0,)), ((), ())), preferred_element_type=F32)


def mm_t(a, b):
    return lax.dot_general(a, b, (((1,), (1,)), ((), ())), preferred_element_type=F32)


def t_mm(a, b):
    return lax.dot_general(a, b, (((0,), (0,)), ((), ())), preferred_element_type=F32)


def rounded(v):
    return v.astype(BF16).astype(F32)


def standard(v):
    centred = v - jnp.mean(v, axis=-1, keepdims=True)
    scale = lax.rsqrt(jnp.mean(centred * centred, axis=-1, keepdims=True) + EPSILON)
    return centred * scale, scale


def norm_pull(grad, gain, xhat, scale):
    d = grad * gain
    return scale * (
        d - jnp.mean(d, axis=-1, keepdims=True) - xhat * jnp.mean(d * xhat, axis=-1, keepdims=True)
    )


def gelu_both(x):
    cdf = 0.5 * (1.0 + lax.erf(x * 0.7071067811865476))
    slope = cdf + x * jnp.exp(-0.5 * x * x) * 0.3989422804014327
    return x * cdf, slope


def attend(q, k, v, mask):
    e = jnp.exp(mm_t(q, k) * SCALE)
    if mask is not None:
        e = e * mask
    p = e * (1.0 / jnp.sum(e, axis=-1, keepdims=True))
    return p, mm(p.astype(BF16), v)


def attend_pull(q, k, v, p, dm):
    dv = t_mm(p.astype(BF16), dm)
    dp = rounded(mm_t(dm, v))
    ds = (p * (dp - jnp.sum(dp * p, axis=-1, keepdims=True)) * SCALE).astype(BF16)
    return mm(ds, k), t_mm(ds, q), dv


def loop(count, body):
    def step(i, carry):
        body(i)
        return carry

    lax.fori_loop(0, count, step, 0)


def chunk(i, size):
    return pl.ds(pl.multiple_of(i * size, size), size)


MERGE, TRIPLE, OUTPUT, UP, DOWN = range(5)
SLOTS = 17


class Gather:
    def __init__(self, shards, full, local_sem, send_sem, recv_sem):
        self.shards, self.full = shards, full
        self.local_sem, self.send_sem, self.recv_sem = local_sem, send_sem, recv_sem
        lat, lon = lax.axis_index("lat"), lax.axis_index("lon")
        self.z, self.xl = lat // 2, lat % 2
        self.y, self.xh, self.c = lon // 4, (lon // 2) % 2, lon % 2
        self.lat, self.lon = lat, lon
        self.up = (self.y + 1) % 4
        self.dn = (self.y + 3) % 4
        self.op = (self.y + 2) % 4
        self.copies = {}
        self.local = {}

    def begin(self):
        for a in range(5):
            here = self.full[a].at[self.y, self.xh, self.c]
            self.local[a] = pltpu.make_async_copy(self.shards[a], here, self.local_sem.at[a])
            self.local[a].start()

    def place(self, z, xl, y, xh, c):
        return {"lat": z * 2 + xl, "lon": y * 4 + xh * 2 + c}

    def neighbours(self):
        z, xl, y, xh, c = self.z, self.xl, self.y, self.xh, self.c
        return [
            self.place(z, 1 - xl, y, 1 - xh, c),
            self.place(z, xl, self.up, xh, c),
            self.place(z, xl, self.dn, xh, c),
            self.place((z + 1) % 8, xl, y, xh, c),
            self.place((z + 7) % 8, xl, y, xh, c),
            self.place(z, xl, y, xh, 1 - c),
        ]

    def half(self, a):
        size = self.shards[a].shape[0] // 2
        return pl.ds(pl.multiple_of((self.z % 2) * size, size), size)

    def send(self, a, slot, src, dst, who):
        copy = pltpu.make_async_remote_copy(
            src_ref=src,
            dst_ref=dst,
            send_sem=self.send_sem.at[a, slot],
            recv_sem=self.recv_sem.at[a, slot],
            device_id=self.neighbours()[who],
            device_id_type=MESH,
        )
        copy.start()
        self.copies[a, slot] = copy

    def got(self, a, slot):
        self.copies[a, slot].wait_recv()

    def tick(self, step, a):
        full, half = self.full[a], self.half(a)
        y, xh, c, up, dn, op = self.y, self.xh, self.c, self.up, self.dn, self.op
        if step == 0:
            self.local[a].wait()
            self.send(a, 0, full.at[y, xh, c], full.at[y, xh, c], 0)
            piece = full.at[y, xh, c, half]
            self.send(a, 1, piece, piece, 1)
            self.send(a, 2, piece, piece, 2)
        elif step == 1:
            self.got(a, 0)
            other = full.at[y, 1 - xh, c, half]
            self.send(a, 3, other, other, 1)
            self.send(a, 4, other, other, 2)
            self.send(a, 13, full.at[y, :, c], full.at[y, :, c], 5)
        elif step == 2:
            for slot, far, pick, who in ((5, dn, 0, 1), (6, up, 1, 2)):
                self.got(a, slot - 4)
                self.got(a, slot - 2)
                piece = full.at[far, pick, c, half]
                self.send(a, slot, piece, piece, who)
                base = 7 + 2 * (slot - 5)
                for d in (0, 1):
                    piece = full.at[far, d, c, half]
                    self.send(a, base + d, piece, piece, 3 + d)
        elif step == 3:
            for d in (0, 1):
                self.got(a, 5 + d)
                piece = full.at[op, d, c, half]
                self.send(a, 11 + d, piece, piece, 3 + d)
        elif step in (4, 5):
            for i, far in (((0, dn), (1, up)), ((2, op),))[step - 4]:
                self.got(a, 7 + 2 * i)
                self.got(a, 8 + 2 * i)
                piece = full.at[far, :, c]
                self.send(a, 14 + i, piece, piece, 5)
        else:
            self.got(a, 13 + step - 6)

    def finish(self):
        for copy in self.copies.values():
            copy.wait_send()


M, T, O, U, D = range(5)
POINTS = {
    "start": [(0, M), (0, O), (0, T), (0, U)],
    "rolled": [(1, M), (1, O)],
    "attention": [(2, M)],
    "down": [(0, D), (1, T), (2, O), (4, M), (3, M)],
    "merge": [(4, O), (2, T), (5, M), (3, O), (6, M), (7, M), (8, M), (9, M)],
    "coarse": [(1, U), (3, T), (6, T)],
    "coarse 1": [(4, T), (7, T), (8, T)],
    "coarse 2": [(5, O), (2, U), (1, D), (5, T)],
    "coarse 3": [(9, T)],
    "coarse out": [(3, U), (6, O), (7, O), (8, O), (9, O)],
    "hidden": [(4, U), (2, D), (6, U), (6, D)],
    "hidden 1": [(5, U), (3, D), (4, D), (7, U), (7, D)],
    "hidden 2": [(5, D), (8, U), (8, D)],
    "hidden 3": [(9, U), (9, D)],
}


def kernel(*refs):
    (
        tok, label_row, g1, wt, wo, g2, wu, wd, gm, s_merge, cg1, s_triple, s_output, cg2, s_up, s_down,
        skip_cot, coarse_cot,
        m_tok_pack, m_tok_own, m_roll_got, m_join_pack, m_join_own, m_back_pack, m_back_own, m_back_got,
        m_back_own_join, m_back_got_join, m_tok_join, m_tok_win,
        skip_out, coarse_out, grad_out,
        f_merge, f_triple, f_output, f_up, f_down,
        x_ref, n_ref, lab_ref, qkv_ref, p_ref, mix_ref, res_ref, act_ref, slope_ref, win_ref,
        grad_ref, dres_ref, dqkv_ref,
        j_ref, nj_ref, mg_ref, cn_ref, cqkv_ref, cp_ref, cmix_ref, cres_ref, cot_ref, hid_ref, dn_ref, cdqkv_ref,
        halo_send, halo_recv, local_sem, send_sem, recv_sem, halo_ssem, halo_rsem,
    ) = refs
    gather = Gather(
        (s_merge, s_triple, s_output, s_up, s_down), (f_merge, f_triple, f_output, f_up, f_down),
        local_sem, send_sem, recv_sem,
    )
    lat, lon = gather.lat, gather.lon
    north, south, west, east = (lat + 15) % 16, (lat + 1) % 16, (lon + 15) % 16, (lon + 1) % 16
    ahead = [{"lat": north, "lon": lon}, {"lat": lat, "lon": west}, {"lat": north, "lon": west}]
    behind = [{"lat": south, "lon": lon}, {"lat": lat, "lon": east}, {"lat": south, "lon": east}]
    everyone = gather.neighbours() + ahead + behind

    gather.begin()
    barrier = pltpu.get_barrier_semaphore()
    for who in everyone:
        pl.semaphore_signal(barrier, inc=1, device_id=who, device_id_type=MESH)
    pl.semaphore_wait(barrier, len(everyone))

    def point(name):
        for step, a in POINTS[name]:
            gather.tick(step, a)

    def exchange(k, value, targets):
        halo_send[k] = value.astype(BF16)
        copies = []
        for i, (first, size) in enumerate(PARTS):
            rows = pl.ds(first, size)
            copy = pltpu.make_async_remote_copy(
                src_ref=halo_send.at[k, rows],
                dst_ref=halo_recv.at[k, rows],
                send_sem=halo_ssem.at[k, i],
                recv_sem=halo_rsem.at[k, i],
                device_id=targets[i],
                device_id_type=MESH,
            )
            copy.start()
            copies.append(copy)
        return copies

    def settle(copies):
        for copy in copies:
            copy.wait()

    copies = exchange(0, mm(m_tok_pack[...], tok[...]), ahead)
    point("start")
    each = lax.broadcasted_iota(jnp.int32, (8, TOKENS), 0)
    lab_ref[...] = mm_t(m_tok_win[...], jnp.where(each == label_row[...], 1.0, 0.0).astype(BF16))
    x_ref[...] = mm(m_tok_own[...], tok[...])
    point("rolled")
    settle(copies)
    x_ref[...] += mm(m_roll_got[...], halo_recv[0])

    def first_norm(i):
        rows = chunk(i, 96)
        n_ref[rows] = (standard(x_ref[rows])[0] * g1[...]).astype(BF16)

    loop(3, first_norm)

    def project(i):
        cols = chunk(i, 256)
        qkv_ref[:, cols] = rounded(mm(n_ref[...], wt[:, cols]))

    loop(6, project)

    def fine_attention(w):
        rows = chunk(w, WIN)
        seen = lab_ref[rows].astype(BF16)
        mask = mm_t(seen, seen)
        for pair in range(4):
            mixed = []
            for h in (2 * pair, 2 * pair + 1):
                q, k, v = (
                    qkv_ref[rows, h * 192 + 64 * i : h * 192 + 64 * i + 64].astype(BF16) for i in range(3)
                )
                p, m = attend(q, k, v, mask)
                p_ref[w * 8 + h] = p
                mixed.append(m)
            mix_ref[rows, pair * 128 : pair * 128 + 128] = jnp.concatenate(mixed, axis=-1)

    loop(4, fine_attention)
    point("attention")

    def out_project(i):
        cols = chunk(i, 256)
        res_ref[:, cols] = x_ref[:, cols] + mm(mix_ref[...].astype(BF16), wo[:, cols])

    loop(2, out_project)

    def second_norm(i):
        rows = chunk(i, 96)
        n_ref[rows] = (standard(res_ref[rows])[0] * g2[...]).astype(BF16)

    loop(3, second_norm)

    def lift(i):
        cols = chunk(i, 256)
        active, slope = gelu_both(mm(n_ref[...], wu[:, cols]))
        act_ref[:, cols] = active.astype(BF16)
        slope_ref[:, cols] = slope.astype(BF16)

    loop(8, lift)

    def lower(i):
        cols = chunk(i, 256)
        win_ref[:, cols] = (res_ref[:, cols] + mm(act_ref[...], wd[:, cols])).astype(BF16)

    loop(2, lower)
    copies = exchange(1, mm(m_back_pack[...], win_ref[...]), behind)
    point("down")
    j_ref[...] = mm(m_back_own_join[...], win_ref[...])
    x_kept = mm(m_back_own[...], win_ref[...])
    settle(copies)
    j_ref[...] += mm(m_back_got_join[...], halo_recv[1])
    skip_out[...] = (x_kept + mm(m_back_got[...], halo_recv[1])).astype(BF16)

    quads = [pl.ds(q * WIN, WIN) for q in range(4)]

    def joined_standard():
        average = sum(jnp.sum(j_ref[q], axis=-1, keepdims=True) for q in quads) * (1.0 / 2048)
        square = 0.0
        for q in quads:
            centred = j_ref[q] - average
            square = square + jnp.sum(centred * centred, axis=-1, keepdims=True)
        return average, lax.rsqrt(square * (1.0 / 2048) + EPSILON)

    average, merge_scale = joined_standard()
    for i, q in enumerate(quads):
        nj_ref[:, i * 512 : i * 512 + 512] = (
            (j_ref[q] - average) * merge_scale * gm[:, i * 512 : i * 512 + 512]
        ).astype(BF16)
    for i in range(6):
        cot_ref[i * 12 : i * 12 + 12] = coarse_cot[i].astype(F32)
    point("merge")

    def merge(i):
        cols = chunk(i, 256)
        weight = f_merge[:, :, :, :, cols].reshape(2048, 256)
        mg_ref[:, cols] = rounded(mm(nj_ref[...], weight))

    loop(4, merge)

    xhat, scale = standard(mg_ref[...])
    cn_ref[...] = (xhat * cg1[...]).astype(BF16)
    order = (gather.y, gather.dn, gather.up, gather.op)

    def coarse_attention(y):
        mixed = []
        packed = mm_t(cn_ref[...], f_triple[y].reshape(768, 1024))
        cqkv_ref[y] = packed
        for i in range(4):
            part = packed[:, i * 192 : i * 192 + 192].astype(BF16)
            p, m = attend(part[:, :64], part[:, 64:128], part[:, 128:], None)
            cp_ref[y * 4 + i] = p
            mixed.append(m)
        cmix_ref[:, chunk(y, 256)] = jnp.concatenate(mixed, axis=-1).astype(BF16)

    for name, y in zip(("coarse", "coarse 1", "coarse 2", "coarse 3"), order):
        point(name)
        coarse_attention(y)
    point("coarse out")

    def coarse_project(i):
        cols = chunk(i, 256)
        weight = f_output[:, :, :, :, cols].reshape(1024, 256)
        cres_ref[:, cols] = mg_ref[:, cols] + mm(cmix_ref[...], weight)

    loop(4, coarse_project)
    xhat, scale = standard(cres_ref[...])
    cn_ref[...] = (xhat * cg2[...]).astype(BF16)
    hid_ref[...] = cres_ref[...]
    dn_ref[...] = jnp.zeros_like(dn_ref)

    def coarse_hidden(y):
        lower_weight = f_down[y].reshape(1024, 1024)
        grad = rounded(mm_t(cot_ref[...].astype(BF16), lower_weight))
        active = []
        total = dn_ref[...]
        for i in range(4):
            upper = f_up[y, i // 2, i % 2]
            value, slope = gelu_both(mm(cn_ref[...], upper))
            active.append(value.astype(BF16))
            total = total + mm_t((grad[:, i * 256 : i * 256 + 256] * slope).astype(BF16), upper)
        dn_ref[...] = total
        hid_ref[...] += mm(jnp.concatenate(active, axis=-1), lower_weight)

    for name, y in zip(("hidden", "hidden 1", "hidden 2", "hidden 3"), order):
        point(name)
        coarse_hidden(y)
    for i in range(6):
        coarse_out[i] = hid_ref[i * 12 : i * 12 + 12].astype(BF16)
    xhat, scale = standard(cres_ref[...])
    cres_ref[...] = cot_ref[...] + norm_pull(dn_ref[...], cg2[...], xhat, scale)

    def coarse_mix_pull(i):
        rows_of = f_output[i].reshape(256, 1024)
        cmix_ref[:, chunk(i, 256)] = mm_t(cres_ref[...].astype(BF16), rows_of).astype(BF16)

    loop(4, coarse_mix_pull)
    dn_ref[...] = jnp.zeros_like(dn_ref)

    def coarse_attention_pull(y):
        dmix = cmix_ref[:, chunk(y, 256)]
        packed = []
        for i in range(4):
            part = cqkv_ref[y, :, i * 192 : i * 192 + 192].astype(BF16)
            packed.extend(
                attend_pull(
                    part[:, :64], part[:, 64:128], part[:, 128:], cp_ref[y * 4 + i], dmix[:, i * 64 : i * 64 + 64]
                )
            )
        packed = jnp.concatenate(packed, axis=-1).astype(BF16)
        dn_ref[...] += mm(packed, f_triple[y].reshape(768, 1024))

    loop(4, coarse_attention_pull)
    xhat, scale = standard(mg_ref[...])
    cn_ref[...] = (cres_ref[...] + norm_pull(dn_ref[...], cg1[...], xhat, scale)).astype(BF16)

    def merge_pull(y):
        res_rows = chunk(y, WIN)
        grad_ref[res_rows] = rounded(mm_t(cn_ref[...], f_merge[y].reshape(512, 1024)))

    loop(4, merge_pull)
    first = 0.0
    second = 0.0
    for i, q in enumerate(quads):
        d = grad_ref[q] * gm[:, i * 512 : i * 512 + 512]
        first = first + jnp.sum(d, axis=-1, keepdims=True)
        second = second + jnp.sum(d * (j_ref[q] - average), axis=-1, keepdims=True)
    first = first * (1.0 / 2048)
    second = second * merge_scale * (1.0 / 2048)
    dqkv_ref[:, :512] = mm(m_tok_join[...], skip_cot[...])
    for i, q in enumerate(quads):
        d = grad_ref[q] * gm[:, i * 512 : i * 512 + 512]
        xhat = (j_ref[q] - average) * merge_scale
        grad_ref[q] = dqkv_ref[q, :512] + merge_scale * (d - first - xhat * second)

    win_ref[...] = grad_ref[...].astype(BF16)
    copies = exchange(2, mm(m_join_pack[...], win_ref[...]), ahead)
    grad_ref[...] = mm(m_join_own[...], win_ref[...])
    settle(copies)
    grad_ref[...] += mm(m_roll_got[...], halo_recv[2])

    def lower_pull(i):
        cols = chunk(i, 256)
        grad = rounded(mm_t(grad_ref[...].astype(BF16), wd[cols]))
        act_ref[:, cols] = (grad * slope_ref[:, cols].astype(F32)).astype(BF16)

    loop(8, lower_pull)

    def lift_pull(i):
        rows = chunk(i, 256)
        dres_ref[:, rows] = rounded(mm_t(act_ref[...], wu[rows]))

    loop(2, lift_pull)

    def second_pull(i):
        rows = chunk(i, 96)
        xhat, scale = standard(res_ref[rows])
        total = grad_ref[rows] + norm_pull(dres_ref[rows], g2[...], xhat, scale)
        dres_ref[rows] = total
        n_ref[rows] = total.astype(BF16)

    loop(3, second_pull)

    def out_pull(i):
        rows = chunk(i, 256)
        mix_ref[:, rows] = rounded(mm_t(n_ref[...], wo[rows]))

    loop(2, out_pull)

    def fine_attention_pull(w):
        rows = chunk(w, WIN)
        for pair in range(4):
            packed = []
            for h in (2 * pair, 2 * pair + 1):
                q, k, v = (
                    qkv_ref[rows, h * 192 + 64 * i : h * 192 + 64 * i + 64].astype(BF16) for i in range(3)
                )
                dm = mix_ref[rows, h * 64 : h * 64 + 64].astype(BF16)
                packed.extend(attend_pull(q, k, v, p_ref[w * 8 + h], dm))
            dqkv_ref[rows, pair * 384 : pair * 384 + 384] = jnp.concatenate(packed, axis=-1)

    loop(4, fine_attention_pull)

    def project_pull(i):
        rows = chunk(i, 256)
        grad_ref[:, rows] = rounded(mm_t(dqkv_ref[...].astype(BF16), wt[rows]))

    loop(2, project_pull)

    def first_pull(i):
        rows = chunk(i, 96)
        xhat, scale = standard(x_ref[rows])
        win_ref[rows] = (dres_ref[rows] + norm_pull(grad_ref[rows], g1[...], xhat, scale)).astype(BF16)

    loop(3, first_pull)
    copies = exchange(3, mm(m_back_pack[...], win_ref[...]), behind)
    grad_ref[...] = mm(m_back_own[...], win_ref[...])
    gather.finish()
    settle(copies)
    grad_out[...] = (grad_ref[...] + mm(m_back_got[...], halo_recv[3])).astype(BF16)


def place_results(*refs):
    for i in range(3):
        refs[3 + i][...] = refs[i][...]


def local(
    fine_tokens, region_labels, g1, wt, wo, g2, wu, wd, gm, s_merge, cg1, s_triple, s_output, cg2, s_up, s_down,
    skip_cot, coarse_cot,
):
    label_row = region_labels.reshape(1, TOKENS)
    moves = [jnp.asarray(m) for m in tables()]
    vmem = pl.BlockSpec(memory_space=pltpu.VMEM)
    held = pl.BlockSpec(memory_space=pl.ANY)
    s_triple = s_triple.T
    shards = (s_merge, s_triple, s_output, s_up, s_down)
    args = [
        fine_tokens.reshape(TOKENS, 512), label_row, g1[None], wt, wo, g2[None], wu, wd, gm[None], s_merge, cg1[None],
        s_triple, s_output, cg2[None], s_up, s_down, skip_cot.reshape(TOKENS, 512), coarse_cot, *moves,
    ]
    in_specs = [held if any(a is s for s in shards) else vmem for a in args]
    f32 = lambda *shape: pltpu.VMEM(shape, F32)
    bf16 = lambda *shape: pltpu.VMEM(shape, BF16)
    scratch = [bf16(4, 2, 2, *s.shape) for s in shards]
    scratch += [
        f32(288, 512), bf16(288, 512), f32(288, 8), f32(288, 1536), f32(32, 72, 72), f32(288, 512),
        f32(288, 512), bf16(288, 2048), bf16(288, 2048), bf16(288, 512),
        f32(288, 512), f32(288, 512), f32(288, 1536),
        f32(288, 512), bf16(72, 2048), f32(72, 1024), bf16(72, 1024), f32(4, 72, 768), f32(16, 72, 72),
        bf16(72, 1024), f32(72, 1024), f32(72, 1024), f32(72, 1024), f32(72, 1024), f32(8, 128),
        bf16(4, HALO, 512), bf16(4, HALO, 512),
        pltpu.SemaphoreType.DMA((5,)), pltpu.SemaphoreType.DMA((5, SLOTS)), pltpu.SemaphoreType.DMA((5, SLOTS)),
        pltpu.SemaphoreType.DMA((4, 3)), pltpu.SemaphoreType.DMA((4, 3)),
    ]
    skip, coarse, grad = pl.pallas_call(
        kernel,
        out_shape=[
            jax.ShapeDtypeStruct((TOKENS, 512), BF16),
            jax.ShapeDtypeStruct((6, 12, 1024), BF16),
            jax.ShapeDtypeStruct((TOKENS, 512), BF16),
        ],
        in_specs=in_specs,
        out_specs=[vmem] * 3,
        scratch_shapes=scratch,
        compiler_params=pltpu.CompilerParams(
            collective_id=0, has_side_effects=True, vmem_limit_bytes=60 * 1024 * 1024
        ),
        name="backbone",
    )(*args)
    skip, coarse, grad = pl.pallas_call(
        place_results,
        out_shape=[jax.ShapeDtypeStruct(a.shape, a.dtype) for a in (skip, coarse, grad)],
        in_specs=[vmem] * 3,
        out_specs=[vmem] * 3,
        name="results",
    )(skip, coarse, grad)
    return skip.reshape(ROWS, COLS, 512), coarse, grad.reshape(ROWS, COLS, 512)


def solution(mesh):
    in_specs = (
        P("lat", "lon", None), P("lat", "lon"), P(), P(), P(), P(), P(), P(), P(), P("lon", None), P(),
        P(None, "lon"), P("lon", None), P(), P(None, "lon"), P("lon", None),
        P("lat", "lon", None), P("lat", "lon", None),
    )
    out_specs = (P("lat", "lon", None), P("lat", "lon", None), P("lat", "lon", None))
    return jax.shard_map(local, mesh=mesh, in_specs=in_specs, out_specs=out_specs, check_vma=False)
```

```python
import functools

import jax
import jax.numpy as jnp
import ml_dtypes
import numpy as np
from jax import lax
from jax.experimental import pallas as pl
from jax.experimental.pallas import tpu as pltpu
from jax.sharding import PartitionSpec as P

MESH = pl.DeviceIdType.MESH
F32 = jnp.float32
BF16 = jnp.bfloat16
EPSILON = 1e-05
SCALE = 0.125
ROWS, COLS = 12, 24
TOKENS = ROWS * COLS
WIN = 72
HALO = 160
PARTS = ((0, 64), (64, 64), (128, 32))


def tok_index(r, c):
    return r * COLS + c


def win_index(r, c):
    return ((r // 6) * 2 + c // 12) * WIN + (r % 6) * 12 + c % 12


def join_index(r, c):
    return (2 * (c % 2) + r % 2) * WIN + (r // 2) * 12 + c // 2


@functools.cache
def tables():
    def forward(source):
        pack = np.zeros((HALO, TOKENS), np.float32)
        own = np.zeros((TOKENS, TOKENS), np.float32)
        got = np.zeros((TOKENS, HALO), np.float32)
        for r in range(ROWS):
            for c in range(COLS):
                far_r, far_c = r + 3 >= ROWS, c + 6 >= COLS
                at = source((r + 3) % ROWS, (c + 6) % COLS)
                if not far_r and not far_c:
                    own[win_index(r, c), at] = 1
                    continue
                if far_r and not far_c:
                    slot = (r - 9) * 18 + c
                elif far_c and not far_r:
                    slot = 64 + r * 6 + (c - 18)
                else:
                    slot = 128 + (r - 9) * 6 + (c - 18)
                pack[slot, at] = 1
                got[win_index(r, c), slot] = 1
        return pack, own, got

    def back(target):
        pack = np.zeros((HALO, TOKENS), np.float32)
        own = np.zeros((TOKENS, TOKENS), np.float32)
        got = np.zeros((TOKENS, HALO), np.float32)
        for r in range(ROWS):
            for c in range(COLS):
                far_r, far_c = r < 3, c < 6
                at = win_index((r - 3) % ROWS, (c - 6) % COLS)
                if not far_r and not far_c:
                    own[target(r, c), at] = 1
                    continue
                if far_r and not far_c:
                    slot = r * 18 + (c - 6)
                elif far_c and not far_r:
                    slot = 64 + (r - 3) * 6 + c
                else:
                    slot = 128 + r * 6 + c
                pack[slot, at] = 1
                got[target(r, c), slot] = 1
        return pack, own, got

    def plain(target):
        move = np.zeros((TOKENS, TOKENS), np.float32)
        for r in range(ROWS):
            for c in range(COLS):
                move[target(r, c), tok_index(r, c)] = 1
        return move

    tok_pack, tok_own, roll_got = forward(tok_index)
    join_pack, join_own, _ = forward(join_index)
    back_pack, back_own, back_got = back(tok_index)
    _, back_own_join, back_got_join = back(join_index)
    every = (
        tok_pack, tok_own, roll_got, join_pack, join_own, back_pack, back_own, back_got,
        back_own_join, back_got_join, plain(join_index), plain(win_index),
    )
    return tuple(m.astype(ml_dtypes.bfloat16) for m in every)


def mm(a, b):
    return lax.dot_general(a, b, (((1,), (0,)), ((), ())), preferred_element_type=F32)


def mm_t(a, b):
    return lax.dot_general(a, b, (((1,), (1,)), ((), ())), preferred_element_type=F32)


def rounded(v):
    return v.astype(BF16).astype(F32)


def standard(v):
    centred = v - jnp.mean(v, axis=-1, keepdims=True)
    scale = lax.rsqrt(jnp.mean(centred * centred, axis=-1, keepdims=True) + EPSILON)
    return centred * scale, scale


def norm_pull(grad, gain, xhat, scale):
    d = grad * gain
    return scale * (
        d - jnp.mean(d, axis=-1, keepdims=True) - xhat * jnp.mean(d * xhat, axis=-1, keepdims=True)
    )


def gelu_both(x):
    cdf = 0.5 * (1.0 + lax.erf(x * 0.7071067811865476))
    slope = cdf + x * jnp.exp(-0.5 * x * x) * 0.3989422804014327
    return x * cdf, slope


def attend(q, k, v, mask):
    e, turned = jnp.exp(mm_t(q, k) * SCALE), jnp.exp(mm_t(k, q) * SCALE)
    if mask is not None:
        e, turned = e * mask, turned * mask
    p = e * (1.0 / jnp.sum(e, axis=-1, keepdims=True))
    turned = turned * (1.0 / jnp.sum(turned, axis=0, keepdims=True))
    return p, turned, mm(p.astype(BF16), v)


def attend_pull(q, k, v, p, turned, dm):
    dv = mm(turned.astype(BF16), dm)
    dp, dp_turned = rounded(mm_t(dm, v)), rounded(mm_t(v, dm))
    ds = p * (dp - jnp.sum(dp * p, axis=-1, keepdims=True)) * SCALE
    ds_turned = turned * (dp_turned - jnp.sum(dp_turned * turned, axis=0, keepdims=True)) * SCALE
    return mm(ds.astype(BF16), k), mm(ds_turned.astype(BF16), q), dv


def loop(count, body):
    def step(i, carry):
        body(i)
        return carry

    lax.fori_loop(0, count, step, 0)


def chunk(i, size):
    return pl.ds(pl.multiple_of(i * size, size), size)


MERGE, TRIPLE, OUTPUT, UP, DOWN = range(5)
SLOTS = 21
QUARTERED = (TRIPLE, OUTPUT)


class Gather:
    def __init__(self, shards, full, local_sem, send_sem, recv_sem):
        self.shards, self.full = shards, full
        self.local_sem, self.send_sem, self.recv_sem = local_sem, send_sem, recv_sem
        lat, lon = lax.axis_index("lat"), lax.axis_index("lon")
        self.z, self.xl = lat // 2, lat % 2
        self.y, self.xh, self.c = lon // 4, (lon // 2) % 2, lon % 2
        self.lat, self.lon = lat, lon
        self.up = (self.y + 1) % 4
        self.dn = (self.y + 3) % 4
        self.op = (self.y + 2) % 4
        self.copies = {}
        self.local = {}

    def begin(self):
        for a in range(5):
            here = self.full[a].at[self.y, self.xh, self.c]
            self.local[a] = pltpu.make_async_copy(self.shards[a], here, self.local_sem.at[a])
            self.local[a].start()

    def place(self, z, xl, y, xh, c):
        return {"lat": z * 2 + xl, "lon": y * 4 + xh * 2 + c}

    def neighbours(self):
        z, xl, y, xh, c = self.z, self.xl, self.y, self.xh, self.c
        return [
            self.place(z, 1 - xl, y, 1 - xh, c),
            self.place(z, xl, self.up, xh, c),
            self.place(z, xl, self.dn, xh, c),
            self.place((z + 1) % 8, xl, y, xh, c),
            self.place((z + 7) % 8, xl, y, xh, c),
            self.place(z, xl, y, xh, 1 - c),
            self.place(z, 1 - xl, y, xh, c),
        ]

    def half(self, a, which):
        size = self.shards[a].shape[0] // 2
        return pl.ds(pl.multiple_of(which * size, size), size)

    def share(self, a):
        if a not in QUARTERED:
            return self.half(a, self.z % 2)
        size = self.shards[a].shape[0] // 4
        return pl.ds(pl.multiple_of((self.xl * 2 + self.z % 2) * size, size), size)

    def send(self, a, slot, src, dst, who):
        copy = pltpu.make_async_remote_copy(
            src_ref=src,
            dst_ref=dst,
            send_sem=self.send_sem.at[a, slot],
            recv_sem=self.recv_sem.at[a, slot],
            device_id=self.neighbours()[who],
            device_id_type=MESH,
        )
        copy.start()
        self.copies[a, slot] = copy

    def got(self, a, slot):
        self.copies[a, slot].wait_recv()

    def tick(self, step, a):
        full, half = self.full[a], self.share(a)
        y, xh, c, up, dn, op = self.y, self.xh, self.c, self.up, self.dn, self.op
        if step == 0:
            self.local[a].wait()
            piece = full.at[y, xh, c, self.half(a, 1 - self.xl)]
            self.send(a, 0, piece, piece, 0)
            piece = full.at[y, xh, c, half]
            self.send(a, 1, piece, piece, 1)
            self.send(a, 2, piece, piece, 2)
        elif step == 10:
            self.got(a, 0)
            piece = full.at[y, 1 - xh, c, self.half(a, self.xl)]
            self.send(a, 17, piece, piece, 6)
        elif step == 1:
            self.got(a, 17)
            other = full.at[y, 1 - xh, c, half]
            self.send(a, 3, other, other, 1)
            self.send(a, 4, other, other, 2)
            self.send(a, 13, full.at[y, :, c], full.at[y, :, c], 5)
        elif step == 2:
            for slot, far, pick, who in ((5, dn, 0, 1), (6, up, 1, 2)):
                self.got(a, slot - 4)
                self.got(a, slot - 2)
                piece = full.at[far, pick, c, half]
                self.send(a, slot, piece, piece, who)
                base = 7 + 2 * (slot - 5)
                for d in (0, 1):
                    piece = full.at[far, d, c, half]
                    self.send(a, base + d, piece, piece, 3 + d)
        elif step == 3:
            for d in (0, 1):
                self.got(a, 5 + d)
                piece = full.at[op, d, c, half]
                self.send(a, 11 + d, piece, piece, 3 + d)
        elif step in (4, 5):
            for i, far in (((0, dn), (1, up)), ((2, op),))[step - 4]:
                self.got(a, 7 + 2 * i)
                self.got(a, 8 + 2 * i)
                if a in QUARTERED:
                    piece = full.at[far, :, c, self.half(a, self.xl)]
                    self.send(a, 18 + i, piece, piece, 6)
                else:
                    piece = full.at[far, :, c]
                    self.send(a, 14 + i, piece, piece, 5)
        elif step in (11, 12):
            for i, far in (((0, dn), (1, up)), ((2, op),))[step - 11]:
                self.got(a, 18 + i)
                piece = full.at[far, :, c]
                self.send(a, 14 + i, piece, piece, 5)
        else:
            self.got(a, 13 + step - 6)

    def finish(self):
        for copy in self.copies.values():
            copy.wait_send()


M, T, O, U, D = range(5)
POINTS = {
    "start": [(0, M), (0, T), (0, O)],
    "rolled": [(10, M), (1, M), (10, T), (0, U)],
    "attention": [(2, M), (1, T), (10, O), (0, D)],
    "down": [(3, M), (2, T), (1, O), (10, U), (4, M), (3, T), (2, O), (1, U)],
    "merge": [(10, D), (5, M), (4, T), (3, O), (2, U), (1, D), (6, M), (7, M), (8, M), (9, M)],
    "coarse": [(5, T), (4, O), (11, T), (6, T)],
    "coarse 1": [(3, U), (2, D), (5, O), (12, T), (7, T), (8, T)],
    "coarse 2": [(11, O), (4, U)],
    "coarse 3": [(3, D), (12, O), (9, T)],
    "coarse out": [(5, U), (6, O), (7, O), (8, O), (9, O)],
    "hidden": [(4, D), (6, U), (6, D)],
    "hidden 1": [(5, D), (7, U), (7, D)],
    "hidden 2": [(8, U), (8, D)],
    "hidden 3": [(9, U), (9, D)],
}


def kernel(*refs):
    (
        tok, label_row, g1, wt, wo, g2, wu, wd, gm, s_merge, cg1, s_triple, s_output, cg2, s_up, s_down,
        skip_cot, coarse_cot,
        m_tok_pack, m_tok_own, m_roll_got, m_join_pack, m_join_own, m_back_pack, m_back_own, m_back_got,
        m_back_own_join, m_back_got_join, m_tok_join, m_tok_win,
        skip_out, coarse_out, grad_out,
        f_merge, f_triple, f_output, f_up, f_down,
        x_ref, n_ref, lab_ref, qkv_ref, p_ref, mix_ref, res_ref, act_ref, slope_ref, win_ref,
        grad_ref, dres_ref, dqkv_ref,
        j_ref, nj_ref, mg_ref, cn_ref, cqkv_ref, cp_ref, cmix_ref, cres_ref, cot_ref, hid_ref, dn_ref,
        pt_ref, cpt_ref,
        halo_send, halo_recv, local_sem, send_sem, recv_sem, halo_ssem, halo_rsem,
    ) = refs
    gather = Gather(
        (s_merge, s_triple, s_output, s_up, s_down), (f_merge, f_triple, f_output, f_up, f_down),
        local_sem, send_sem, recv_sem,
    )
    lat, lon = gather.lat, gather.lon
    north, south, west, east = (lat + 15) % 16, (lat + 1) % 16, (lon + 15) % 16, (lon + 1) % 16
    ahead = [{"lat": north, "lon": lon}, {"lat": lat, "lon": west}, {"lat": north, "lon": west}]
    behind = [{"lat": south, "lon": lon}, {"lat": lat, "lon": east}, {"lat": south, "lon": east}]
    everyone = gather.neighbours() + ahead + behind

    gather.begin()
    barrier = pltpu.get_barrier_semaphore()
    for who in everyone:
        pl.semaphore_signal(barrier, inc=1, device_id=who, device_id_type=MESH)
    pl.semaphore_wait(barrier, len(everyone))

    def point(name):
        for step, a in POINTS[name]:
            gather.tick(step, a)

    def exchange(k, value, targets):
        halo_send[k] = value.astype(BF16)
        copies = []
        for i, (first, size) in enumerate(PARTS):
            rows = pl.ds(first, size)
            copy = pltpu.make_async_remote_copy(
                src_ref=halo_send.at[k, rows],
                dst_ref=halo_recv.at[k, rows],
                send_sem=halo_ssem.at[k, i],
                recv_sem=halo_rsem.at[k, i],
                device_id=targets[i],
                device_id_type=MESH,
            )
            copy.start()
            copies.append(copy)
        return copies

    def settle(copies):
        for copy in copies:
            copy.wait()

    copies = exchange(0, mm(m_tok_pack[...], tok[...]), ahead)
    point("start")
    each = lax.broadcasted_iota(jnp.int32, (8, TOKENS), 0)
    lab_ref[...] = mm_t(m_tok_win[...], jnp.where(each == label_row[...], 1.0, 0.0).astype(BF16))
    x_ref[...] = mm(m_tok_own[...], tok[...])
    point("rolled")
    settle(copies)
    x_ref[...] += mm(m_roll_got[...], halo_recv[0])

    def first_norm(i):
        rows = chunk(i, 96)
        n_ref[rows] = (standard(x_ref[rows])[0] * g1[...]).astype(BF16)

    loop(3, first_norm)

    def project(i):
        cols = chunk(i, 256)
        qkv_ref[:, cols] = rounded(mm(n_ref[...], wt[:, cols]))

    loop(6, project)

    def fine_attention(w):
        rows = chunk(w, WIN)
        seen = lab_ref[rows].astype(BF16)
        mask = mm_t(seen, seen)
        for pair in range(4):
            mixed = []
            for h in (2 * pair, 2 * pair + 1):
                q, k, v = (
                    qkv_ref[rows, h * 192 + 64 * i : h * 192 + 64 * i + 64].astype(BF16) for i in range(3)
                )
                p_ref[w * 8 + h], pt_ref[w * 8 + h], m = attend(q, k, v, mask)
                mixed.append(m)
            mix_ref[rows, pair * 128 : pair * 128 + 128] = jnp.concatenate(mixed, axis=-1)

    loop(4, fine_attention)
    point("attention")

    def out_project(i):
        cols = chunk(i, 256)
        res_ref[:, cols] = x_ref[:, cols] + mm(mix_ref[...].astype(BF16), wo[:, cols])

    loop(2, out_project)

    def second_norm(i):
        rows = chunk(i, 96)
        n_ref[rows] = (standard(res_ref[rows])[0] * g2[...]).astype(BF16)

    loop(3, second_norm)

    def lift(i):
        cols = chunk(i, 256)
        active, slope = gelu_both(mm(n_ref[...], wu[:, cols]))
        act_ref[:, cols] = active.astype(BF16)
        slope_ref[:, cols] = slope.astype(BF16)

    loop(8, lift)

    def lower(i):
        cols = chunk(i, 256)
        win_ref[:, cols] = (res_ref[:, cols] + mm(act_ref[...], wd[:, cols])).astype(BF16)

    loop(2, lower)
    copies = exchange(1, mm(m_back_pack[...], win_ref[...]), behind)
    point("down")
    j_ref[...] = mm(m_back_own_join[...], win_ref[...])
    x_kept = mm(m_back_own[...], win_ref[...])
    settle(copies)
    j_ref[...] += mm(m_back_got_join[...], halo_recv[1])
    skip_out[...] = (x_kept + mm(m_back_got[...], halo_recv[1])).astype(BF16)

    quads = [pl.ds(q * WIN, WIN) for q in range(4)]

    def joined_standard():
        average = sum(jnp.sum(j_ref[q], axis=-1, keepdims=True) for q in quads) * (1.0 / 2048)
        square = 0.0
        for q in quads:
            centred = j_ref[q] - average
            square = square + jnp.sum(centred * centred, axis=-1, keepdims=True)
        return average, lax.rsqrt(square * (1.0 / 2048) + EPSILON)

    average, merge_scale = joined_standard()
    for i, q in enumerate(quads):
        nj_ref[:, i * 512 : i * 512 + 512] = (
            (j_ref[q] - average) * merge_scale * gm[:, i * 512 : i * 512 + 512]
        ).astype(BF16)
    for i in range(6):
        cot_ref[i * 12 : i * 12 + 12] = coarse_cot[i].astype(F32)
    point("merge")

    def merge(i):
        cols = chunk(i, 256)
        weight = f_merge[:, :, :, :, cols].reshape(2048, 256)
        mg_ref[:, cols] = rounded(mm(nj_ref[...], weight))

    loop(4, merge)

    xhat, scale = standard(mg_ref[...])
    cn_ref[...] = (xhat * cg1[...]).astype(BF16)
    order = (gather.y, gather.dn, gather.up, gather.op)

    def coarse_attention(y):
        mixed = []
        packed = mm_t(cn_ref[...], f_triple[y].reshape(768, 1024))
        cqkv_ref[y] = packed
        for i in range(4):
            part = packed[:, i * 192 : i * 192 + 192].astype(BF16)
            p, turned, m = attend(part[:, :64], part[:, 64:128], part[:, 128:], None)
            cp_ref[y * 4 + i] = p
            cpt_ref[y * 4 + i] = turned
            mixed.append(m)
        cmix_ref[:, chunk(y, 256)] = jnp.concatenate(mixed, axis=-1).astype(BF16)

    for name, y in zip(("coarse", "coarse 1", "coarse 2", "coarse 3"), order):
        point(name)
        coarse_attention(y)
    point("coarse out")

    def coarse_project(i):
        cols = chunk(i, 256)
        weight = f_output[:, :, :, :, cols].reshape(1024, 256)
        cres_ref[:, cols] = mg_ref[:, cols] + mm(cmix_ref[...], weight)

    loop(4, coarse_project)
    xhat, scale = standard(cres_ref[...])
    cn_ref[...] = (xhat * cg2[...]).astype(BF16)
    hid_ref[...] = cres_ref[...]
    dn_ref[...] = jnp.zeros_like(dn_ref)

    def coarse_hidden(y):
        lower_weight = f_down[y].reshape(1024, 1024)
        grad = rounded(mm_t(cot_ref[...].astype(BF16), lower_weight))
        active = []
        total = dn_ref[...]
        for i in range(4):
            upper = f_up[y, i // 2, i % 2]
            value, slope = gelu_both(mm(cn_ref[...], upper))
            active.append(value.astype(BF16))
            total = total + mm_t((grad[:, i * 256 : i * 256 + 256] * slope).astype(BF16), upper)
        dn_ref[...] = total
        hid_ref[...] += mm(jnp.concatenate(active, axis=-1), lower_weight)

    for name, y in zip(("hidden", "hidden 1", "hidden 2", "hidden 3"), order):
        point(name)
        coarse_hidden(y)
    for i in range(6):
        coarse_out[i] = hid_ref[i * 12 : i * 12 + 12].astype(BF16)
    xhat, scale = standard(cres_ref[...])
    cres_ref[...] = cot_ref[...] + norm_pull(dn_ref[...], cg2[...], xhat, scale)

    def coarse_mix_pull(i):
        rows_of = f_output[i].reshape(256, 1024)
        cmix_ref[:, chunk(i, 256)] = mm_t(cres_ref[...].astype(BF16), rows_of).astype(BF16)

    loop(4, coarse_mix_pull)
    dn_ref[...] = jnp.zeros_like(dn_ref)

    def coarse_attention_pull(y):
        dmix = cmix_ref[:, chunk(y, 256)]
        packed = []
        for i in range(4):
            part = cqkv_ref[y, :, i * 192 : i * 192 + 192].astype(BF16)
            packed.extend(
                attend_pull(
                    part[:, :64], part[:, 64:128], part[:, 128:], cp_ref[y * 4 + i], cpt_ref[y * 4 + i],
                    dmix[:, i * 64 : i * 64 + 64],
                )
            )
        packed = jnp.concatenate(packed, axis=-1).astype(BF16)
        dn_ref[...] += mm(packed, f_triple[y].reshape(768, 1024))

    loop(4, coarse_attention_pull)
    xhat, scale = standard(mg_ref[...])
    cn_ref[...] = (cres_ref[...] + norm_pull(dn_ref[...], cg1[...], xhat, scale)).astype(BF16)

    def merge_pull(y):
        res_rows = chunk(y, WIN)
        grad_ref[res_rows] = rounded(mm_t(cn_ref[...], f_merge[y].reshape(512, 1024)))

    loop(4, merge_pull)
    first = 0.0
    second = 0.0
    for i, q in enumerate(quads):
        d = grad_ref[q] * gm[:, i * 512 : i * 512 + 512]
        first = first + jnp.sum(d, axis=-1, keepdims=True)
        second = second + jnp.sum(d * (j_ref[q] - average), axis=-1, keepdims=True)
    first = first * (1.0 / 2048)
    second = second * merge_scale * (1.0 / 2048)
    dqkv_ref[:, :512] = mm(m_tok_join[...], skip_cot[...])
    for i, q in enumerate(quads):
        d = grad_ref[q] * gm[:, i * 512 : i * 512 + 512]
        xhat = (j_ref[q] - average) * merge_scale
        grad_ref[q] = dqkv_ref[q, :512] + merge_scale * (d - first - xhat * second)

    win_ref[...] = grad_ref[...].astype(BF16)
    copies = exchange(2, mm(m_join_pack[...], win_ref[...]), ahead)
    grad_ref[...] = mm(m_join_own[...], win_ref[...])
    settle(copies)
    grad_ref[...] += mm(m_roll_got[...], halo_recv[2])

    def lower_pull(i):
        cols = chunk(i, 256)
        grad = rounded(mm_t(grad_ref[...].astype(BF16), wd[cols]))
        act_ref[:, cols] = (grad * slope_ref[:, cols].astype(F32)).astype(BF16)

    loop(8, lower_pull)

    def lift_pull(i):
        rows = chunk(i, 256)
        dres_ref[:, rows] = rounded(mm_t(act_ref[...], wu[rows]))

    loop(2, lift_pull)

    def second_pull(i):
        rows = chunk(i, 96)
        xhat, scale = standard(res_ref[rows])
        total = grad_ref[rows] + norm_pull(dres_ref[rows], g2[...], xhat, scale)
        dres_ref[rows] = total
        n_ref[rows] = total.astype(BF16)

    loop(3, second_pull)

    def out_pull(i):
        rows = chunk(i, 256)
        mix_ref[:, rows] = rounded(mm_t(n_ref[...], wo[rows]))

    loop(2, out_pull)

    def fine_attention_pull(w):
        rows = chunk(w, WIN)
        for pair in range(4):
            packed = []
            for h in (2 * pair, 2 * pair + 1):
                q, k, v = (
                    qkv_ref[rows, h * 192 + 64 * i : h * 192 + 64 * i + 64].astype(BF16) for i in range(3)
                )
                dm = mix_ref[rows, h * 64 : h * 64 + 64].astype(BF16)
                packed.extend(attend_pull(q, k, v, p_ref[w * 8 + h], pt_ref[w * 8 + h], dm))
            dqkv_ref[rows, pair * 384 : pair * 384 + 384] = jnp.concatenate(packed, axis=-1)

    loop(4, fine_attention_pull)

    def project_pull(i):
        rows = chunk(i, 256)
        grad_ref[:, rows] = rounded(mm_t(dqkv_ref[...].astype(BF16), wt[rows]))

    loop(2, project_pull)

    def first_pull(i):
        rows = chunk(i, 96)
        xhat, scale = standard(x_ref[rows])
        win_ref[rows] = (dres_ref[rows] + norm_pull(grad_ref[rows], g1[...], xhat, scale)).astype(BF16)

    loop(3, first_pull)
    copies = exchange(3, mm(m_back_pack[...], win_ref[...]), behind)
    grad_ref[...] = mm(m_back_own[...], win_ref[...])
    gather.finish()
    settle(copies)
    grad_out[...] = (grad_ref[...] + mm(m_back_got[...], halo_recv[3])).astype(BF16)


def place_results(*refs):
    for i in range(3):
        refs[3 + i][...] = refs[i][...]


def local(
    fine_tokens, region_labels, g1, wt, wo, g2, wu, wd, gm, s_merge, cg1, s_triple, s_output, cg2, s_up, s_down,
    skip_cot, coarse_cot,
):
    label_row = region_labels.reshape(1, TOKENS)
    moves = [jnp.asarray(m) for m in tables()]
    vmem = pl.BlockSpec(memory_space=pltpu.VMEM)
    held = pl.BlockSpec(memory_space=pl.ANY)
    s_triple = s_triple.T
    shards = (s_merge, s_triple, s_output, s_up, s_down)
    args = [
        fine_tokens.reshape(TOKENS, 512), label_row, g1[None], wt, wo, g2[None], wu, wd, gm[None], s_merge, cg1[None],
        s_triple, s_output, cg2[None], s_up, s_down, skip_cot.reshape(TOKENS, 512), coarse_cot, *moves,
    ]
    in_specs = [held if any(a is s for s in shards) else vmem for a in args]
    f32 = lambda *shape: pltpu.VMEM(shape, F32)
    bf16 = lambda *shape: pltpu.VMEM(shape, BF16)
    scratch = [bf16(4, 2, 2, *s.shape) for s in shards]
    scratch += [
        f32(288, 512), bf16(288, 512), f32(288, 8), f32(288, 1536), f32(32, 72, 72), f32(288, 512),
        f32(288, 512), bf16(288, 2048), bf16(288, 2048), bf16(288, 512),
        f32(288, 512), f32(288, 512), f32(288, 1536),
        f32(288, 512), bf16(72, 2048), f32(72, 1024), bf16(72, 1024), f32(4, 72, 768), f32(16, 72, 72),
        bf16(72, 1024), f32(72, 1024), f32(72, 1024), f32(72, 1024), f32(72, 1024),
        f32(32, 72, 72), f32(16, 72, 72),
        bf16(4, HALO, 512), bf16(4, HALO, 512),
        pltpu.SemaphoreType.DMA((5,)), pltpu.SemaphoreType.DMA((5, SLOTS)), pltpu.SemaphoreType.DMA((5, SLOTS)),
        pltpu.SemaphoreType.DMA((4, 3)), pltpu.SemaphoreType.DMA((4, 3)),
    ]
    skip, coarse, grad = pl.pallas_call(
        kernel,
        out_shape=[
            jax.ShapeDtypeStruct((TOKENS, 512), BF16),
            jax.ShapeDtypeStruct((6, 12, 1024), BF16),
            jax.ShapeDtypeStruct((TOKENS, 512), BF16),
        ],
        in_specs=in_specs,
        out_specs=[vmem] * 3,
        scratch_shapes=scratch,
        compiler_params=pltpu.CompilerParams(
            collective_id=0, has_side_effects=True, vmem_limit_bytes=60 * 1024 * 1024
        ),
        name="backbone",
    )(*args)
    skip, coarse, grad = pl.pallas_call(
        place_results,
        out_shape=[jax.ShapeDtypeStruct(a.shape, a.dtype) for a in (skip, coarse, grad)],
        in_specs=[vmem] * 3,
        out_specs=[vmem] * 3,
        name="results",
    )(skip, coarse, grad)
    return skip.reshape(ROWS, COLS, 512), coarse, grad.reshape(ROWS, COLS, 512)


def solution(mesh):
    in_specs = (
        P("lat", "lon", None), P("lat", "lon"), P(), P(), P(), P(), P(), P(), P(), P("lon", None), P(),
        P(None, "lon"), P("lon", None), P(), P(None, "lon"), P("lon", None),
        P("lat", "lon", None), P("lat", "lon", None),
    )
    out_specs = (P("lat", "lon", None), P("lat", "lon", None), P("lat", "lon", None))
    return jax.shard_map(local, mesh=mesh, in_specs=in_specs, out_specs=out_specs, check_vma=False)
```

```python
import functools

import jax
import jax.numpy as jnp
import ml_dtypes
import numpy as np
from jax import lax
from jax.experimental import pallas as pl
from jax.experimental.pallas import tpu as pltpu
from jax.sharding import PartitionSpec as P

MESH = pl.DeviceIdType.MESH
F32 = jnp.float32
BF16 = jnp.bfloat16
EPSILON = 1e-05
SCALE = 0.125
ROWS, COLS = 12, 24
TOKENS = ROWS * COLS
WIN = 72
HALO = 160
PARTS = ((0, 64), (64, 64), (128, 32))


def tok_index(r, c):
    return r * COLS + c


def win_index(r, c):
    return ((r // 6) * 2 + c // 12) * WIN + (r % 6) * 12 + c % 12


def join_index(r, c):
    return (2 * (c % 2) + r % 2) * WIN + (r // 2) * 12 + c // 2


@functools.cache
def tables():
    def forward(source):
        pack = np.zeros((HALO, TOKENS), np.float32)
        own = np.zeros((TOKENS, TOKENS), np.float32)
        got = np.zeros((TOKENS, HALO), np.float32)
        for r in range(ROWS):
            for c in range(COLS):
                far_r, far_c = r + 3 >= ROWS, c + 6 >= COLS
                at = source((r + 3) % ROWS, (c + 6) % COLS)
                if not far_r and not far_c:
                    own[win_index(r, c), at] = 1
                    continue
                if far_r and not far_c:
                    slot = (r - 9) * 18 + c
                elif far_c and not far_r:
                    slot = 64 + r * 6 + (c - 18)
                else:
                    slot = 128 + (r - 9) * 6 + (c - 18)
                pack[slot, at] = 1
                got[win_index(r, c), slot] = 1
        return pack, own, got

    def back(target):
        pack = np.zeros((HALO, TOKENS), np.float32)
        own = np.zeros((TOKENS, TOKENS), np.float32)
        got = np.zeros((TOKENS, HALO), np.float32)
        for r in range(ROWS):
            for c in range(COLS):
                far_r, far_c = r < 3, c < 6
                at = win_index((r - 3) % ROWS, (c - 6) % COLS)
                if not far_r and not far_c:
                    own[target(r, c), at] = 1
                    continue
                if far_r and not far_c:
                    slot = r * 18 + (c - 6)
                elif far_c and not far_r:
                    slot = 64 + (r - 3) * 6 + c
                else:
                    slot = 128 + r * 6 + c
                pack[slot, at] = 1
                got[target(r, c), slot] = 1
        return pack, own, got

    def plain(target):
        move = np.zeros((TOKENS, TOKENS), np.float32)
        for r in range(ROWS):
            for c in range(COLS):
                move[target(r, c), tok_index(r, c)] = 1
        return move

    tok_pack, tok_own, roll_got = forward(tok_index)
    join_pack, join_own, _ = forward(join_index)
    back_pack, back_own, back_got = back(tok_index)
    _, back_own_join, back_got_join = back(join_index)
    every = (
        tok_pack, tok_own, roll_got, join_pack, join_own, back_pack, back_own, back_got,
        back_own_join, back_got_join, plain(join_index), plain(win_index),
    )
    return tuple(m.astype(ml_dtypes.bfloat16) for m in every)


def mm(a, b):
    return lax.dot_general(a, b, (((1,), (0,)), ((), ())), preferred_element_type=F32)


def mm_t(a, b):
    return lax.dot_general(a, b, (((1,), (1,)), ((), ())), preferred_element_type=F32)


def rounded(v):
    return v.astype(BF16).astype(F32)


def standard(v):
    centred = v - jnp.mean(v, axis=-1, keepdims=True)
    scale = lax.rsqrt(jnp.mean(centred * centred, axis=-1, keepdims=True) + EPSILON)
    return centred * scale, scale


def norm_pull(grad, gain, xhat, scale):
    d = grad * gain
    return scale * (
        d - jnp.mean(d, axis=-1, keepdims=True) - xhat * jnp.mean(d * xhat, axis=-1, keepdims=True)
    )


def gelu_both(x):
    cdf = 0.5 * (1.0 + lax.erf(x * 0.7071067811865476))
    slope = cdf + x * jnp.exp(-0.5 * x * x) * 0.3989422804014327
    return x * cdf, slope


def attend(q, k, v, mask):
    e, turned = jnp.exp(mm_t(q, k) * SCALE), jnp.exp(mm_t(k, q) * SCALE)
    if mask is not None:
        e, turned = e * mask, turned * mask
    p = e * (1.0 / jnp.sum(e, axis=-1, keepdims=True))
    turned = turned * (1.0 / jnp.sum(turned, axis=0, keepdims=True))
    return p, turned, mm(p.astype(BF16), v)


def attend_pull(q, k, v, p, turned, dm):
    dv = mm(turned.astype(BF16), dm)
    dp, dp_turned = rounded(mm_t(dm, v)), rounded(mm_t(v, dm))
    ds = p * (dp - jnp.sum(dp * p, axis=-1, keepdims=True)) * SCALE
    ds_turned = turned * (dp_turned - jnp.sum(dp_turned * turned, axis=0, keepdims=True)) * SCALE
    return mm(ds.astype(BF16), k), mm(ds_turned.astype(BF16), q), dv


def loop(count, body):
    def step(i, carry):
        body(i)
        return carry

    lax.fori_loop(0, count, step, 0)


def chunk(i, size):
    return pl.ds(pl.multiple_of(i * size, size), size)


MERGE, TRIPLE, OUTPUT, UP, DOWN = range(5)
SLOTS = 21
QUARTERED = (TRIPLE, OUTPUT)


class Gather:
    def __init__(self, shards, full, local_sem, send_sem, recv_sem):
        self.shards, self.full = shards, full
        self.local_sem, self.send_sem, self.recv_sem = local_sem, send_sem, recv_sem
        lat, lon = lax.axis_index("lat"), lax.axis_index("lon")
        self.z, self.xl = lat // 2, lat % 2
        self.y, self.xh, self.c = lon // 4, (lon // 2) % 2, lon % 2
        self.lat, self.lon = lat, lon
        self.up = (self.y + 1) % 4
        self.dn = (self.y + 3) % 4
        self.op = (self.y + 2) % 4
        self.copies = {}
        self.local = {}

    def begin(self):
        for a in range(5):
            here = self.full[a].at[self.y, self.xh, self.c]
            self.local[a] = pltpu.make_async_copy(self.shards[a], here, self.local_sem.at[a])
            self.local[a].start()

    def place(self, z, xl, y, xh, c):
        return {"lat": z * 2 + xl, "lon": y * 4 + xh * 2 + c}

    def neighbours(self):
        z, xl, y, xh, c = self.z, self.xl, self.y, self.xh, self.c
        return [
            self.place(z, 1 - xl, y, 1 - xh, c),
            self.place(z, xl, self.up, xh, c),
            self.place(z, xl, self.dn, xh, c),
            self.place((z + 1) % 8, xl, y, xh, c),
            self.place((z + 7) % 8, xl, y, xh, c),
            self.place(z, xl, y, xh, 1 - c),
            self.place(z, 1 - xl, y, xh, c),
        ]

    def half(self, a, which):
        size = self.shards[a].shape[0] // 2
        return pl.ds(pl.multiple_of(which * size, size), size)

    def share(self, a):
        if a not in QUARTERED:
            return self.half(a, self.z % 2)
        size = self.shards[a].shape[0] // 4
        return pl.ds(pl.multiple_of((self.xl * 2 + self.z % 2) * size, size), size)

    def send(self, a, slot, src, dst, who):
        copy = pltpu.make_async_remote_copy(
            src_ref=src,
            dst_ref=dst,
            send_sem=self.send_sem.at[a, slot],
            recv_sem=self.recv_sem.at[a, slot],
            device_id=self.neighbours()[who],
            device_id_type=MESH,
        )
        copy.start()
        self.copies[a, slot] = copy

    def got(self, a, slot):
        self.copies[a, slot].wait_recv()

    def tick(self, step, a):
        full, half = self.full[a], self.share(a)
        y, xh, c, up, dn, op = self.y, self.xh, self.c, self.up, self.dn, self.op
        if step == 0:
            self.local[a].wait()
            piece = full.at[y, xh, c, self.half(a, 1 - self.xl)]
            self.send(a, 0, piece, piece, 0)
            piece = full.at[y, xh, c, half]
            self.send(a, 1, piece, piece, 1)
            self.send(a, 2, piece, piece, 2)
        elif step == 10:
            self.got(a, 0)
            piece = full.at[y, 1 - xh, c, self.half(a, self.xl)]
            self.send(a, 17, piece, piece, 6)
        elif step == 1:
            self.got(a, 17)
            other = full.at[y, 1 - xh, c, half]
            self.send(a, 3, other, other, 1)
            self.send(a, 4, other, other, 2)
            self.send(a, 13, full.at[y, :, c], full.at[y, :, c], 5)
        elif step == 2:
            for slot, far, pick, who in ((5, dn, 0, 1), (6, up, 1, 2)):
                self.got(a, slot - 4)
                self.got(a, slot - 2)
                piece = full.at[far, pick, c, half]
                self.send(a, slot, piece, piece, who)
                base = 7 + 2 * (slot - 5)
                for d in (0, 1):
                    piece = full.at[far, d, c, half]
                    self.send(a, base + d, piece, piece, 3 + d)
        elif step == 3:
            for d in (0, 1):
                self.got(a, 5 + d)
                piece = full.at[op, d, c, half]
                self.send(a, 11 + d, piece, piece, 3 + d)
        elif step in (4, 5):
            for i, far in (((0, dn), (1, up)), ((2, op),))[step - 4]:
                self.got(a, 7 + 2 * i)
                self.got(a, 8 + 2 * i)
                if a in QUARTERED:
                    piece = full.at[far, :, c, self.half(a, self.xl)]
                    self.send(a, 18 + i, piece, piece, 6)
                else:
                    piece = full.at[far, :, c]
                    self.send(a, 14 + i, piece, piece, 5)
        elif step in (11, 12):
            for i, far in (((0, dn), (1, up)), ((2, op),))[step - 11]:
                self.got(a, 18 + i)
                piece = full.at[far, :, c]
                self.send(a, 14 + i, piece, piece, 5)
        else:
            self.got(a, 13 + step - 6)

    def finish(self):
        for copy in self.copies.values():
            copy.wait_send()


M, T, O, U, D = range(5)
POINTS = {
    "start": [(0, M), (0, T), (0, O)],
    "rolled": [(10, M), (1, M), (10, T), (0, U)],
    "attention": [(2, M), (1, T), (10, O), (0, D)],
    "down": [(3, M), (2, T), (1, O), (10, U), (4, M), (3, T), (2, O), (1, U)],
    "merge": [(10, D), (5, M), (4, T), (3, O), (2, U), (1, D), (6, M), (7, M), (8, M), (9, M)],
    "coarse": [(5, T), (4, O), (11, T), (6, T)],
    "coarse 1": [(3, U), (2, D), (5, O), (12, T), (7, T), (8, T)],
    "coarse 2": [(11, O), (4, U)],
    "coarse 3": [(3, D), (12, O), (9, T)],
    "coarse out": [(5, U), (6, O), (7, O), (8, O), (9, O)],
    "hidden": [(4, D), (6, U), (6, D)],
    "hidden 1": [(5, D), (7, U), (7, D)],
    "hidden 2": [(8, U), (8, D)],
    "hidden 3": [(9, U), (9, D)],
}


def kernel(*refs):
    (
        tok, label_row, g1, wt, wo, g2, wu, wd, gm, s_merge, cg1, s_triple, s_output, cg2, s_up, s_down,
        skip_cot, coarse_cot,
        m_tok_pack, m_tok_own, m_roll_got, m_join_pack, m_join_own, m_back_pack, m_back_own, m_back_got,
        m_back_own_join, m_back_got_join, m_tok_join, m_tok_win,
        skip_out, coarse_out, grad_out,
        f_merge, f_triple, f_output, f_up, f_down,
        x_ref, n_ref, lab_ref, qkv_ref, p_ref, mix_ref, res_ref, act_ref, slope_ref, win_ref,
        grad_ref, dres_ref, dqkv_ref,
        j_ref, nj_ref, mg_ref, cn_ref, cqkv_ref, cp_ref, cmix_ref, cres_ref, cot_ref, hid_ref, dn_ref,
        pt_ref, cpt_ref, lifted_ref,
        halo_send, halo_recv, local_sem, send_sem, recv_sem, halo_ssem, halo_rsem,
    ) = refs
    gather = Gather(
        (s_merge, s_triple, s_output, s_up, s_down), (f_merge, f_triple, f_output, f_up, f_down),
        local_sem, send_sem, recv_sem,
    )
    lat, lon = gather.lat, gather.lon
    north, south, west, east = (lat + 15) % 16, (lat + 1) % 16, (lon + 15) % 16, (lon + 1) % 16
    ahead = [{"lat": north, "lon": lon}, {"lat": lat, "lon": west}, {"lat": north, "lon": west}]
    behind = [{"lat": south, "lon": lon}, {"lat": lat, "lon": east}, {"lat": south, "lon": east}]
    everyone = gather.neighbours() + ahead + behind

    gather.begin()
    barrier = pltpu.get_barrier_semaphore()
    for who in everyone:
        pl.semaphore_signal(barrier, inc=1, device_id=who, device_id_type=MESH)
    pl.semaphore_wait(barrier, len(everyone))

    def point(name):
        for step, a in POINTS[name]:
            gather.tick(step, a)

    def exchange(k, value, targets):
        halo_send[k] = value.astype(BF16)
        copies = []
        for i, (first, size) in enumerate(PARTS):
            rows = pl.ds(first, size)
            copy = pltpu.make_async_remote_copy(
                src_ref=halo_send.at[k, rows],
                dst_ref=halo_recv.at[k, rows],
                send_sem=halo_ssem.at[k, i],
                recv_sem=halo_rsem.at[k, i],
                device_id=targets[i],
                device_id_type=MESH,
            )
            copy.start()
            copies.append(copy)
        return copies

    def settle(copies):
        for copy in copies:
            copy.wait()

    copies = exchange(0, mm(m_tok_pack[...], tok[...]), ahead)
    point("start")
    each = lax.broadcasted_iota(jnp.int32, (8, TOKENS), 0)
    lab_ref[...] = mm_t(m_tok_win[...], jnp.where(each == label_row[...], 1.0, 0.0).astype(BF16))
    x_ref[...] = mm(m_tok_own[...], tok[...])
    point("rolled")
    settle(copies)
    x_ref[...] += mm(m_roll_got[...], halo_recv[0])

    def first_norm(i):
        rows = chunk(i, 96)
        n_ref[rows] = (standard(x_ref[rows])[0] * g1[...]).astype(BF16)

    loop(3, first_norm)

    def project(i):
        cols = chunk(i, 256)
        qkv_ref[:, cols] = rounded(mm(n_ref[...], wt[:, cols]))

    loop(6, project)

    def fine_attention(w):
        rows = chunk(w, WIN)
        seen = lab_ref[rows].astype(BF16)
        mask = mm_t(seen, seen)
        for pair in range(4):
            mixed = []
            for h in (2 * pair, 2 * pair + 1):
                q, k, v = (
                    qkv_ref[rows, h * 192 + 64 * i : h * 192 + 64 * i + 64].astype(BF16) for i in range(3)
                )
                p_ref[w * 8 + h], pt_ref[w * 8 + h], m = attend(q, k, v, mask)
                mixed.append(m)
            mix_ref[rows, pair * 128 : pair * 128 + 128] = jnp.concatenate(mixed, axis=-1)

    loop(4, fine_attention)
    point("attention")

    def out_project(i):
        cols = chunk(i, 256)
        res_ref[:, cols] = x_ref[:, cols] + mm(mix_ref[...].astype(BF16), wo[:, cols])

    loop(2, out_project)

    def second_norm(i):
        rows = chunk(i, 96)
        n_ref[rows] = (standard(res_ref[rows])[0] * g2[...]).astype(BF16)

    loop(3, second_norm)

    def lift(i):
        cols = chunk(i, 256)
        active, slope = gelu_both(mm(n_ref[...], wu[:, cols]))
        act_ref[:, cols] = active.astype(BF16)
        slope_ref[:, cols] = slope.astype(BF16)

    loop(8, lift)

    def lower(i):
        cols = chunk(i, 256)
        win_ref[:, cols] = (res_ref[:, cols] + mm(act_ref[...], wd[:, cols])).astype(BF16)

    loop(2, lower)
    copies = exchange(1, mm(m_back_pack[...], win_ref[...]), behind)
    point("down")
    j_ref[...] = mm(m_back_own_join[...], win_ref[...])
    x_kept = mm(m_back_own[...], win_ref[...])
    settle(copies)
    j_ref[...] += mm(m_back_got_join[...], halo_recv[1])
    skip_out[...] = (x_kept + mm(m_back_got[...], halo_recv[1])).astype(BF16)

    quads = [pl.ds(q * WIN, WIN) for q in range(4)]

    def joined_standard():
        average = sum(jnp.sum(j_ref[q], axis=-1, keepdims=True) for q in quads) * (1.0 / 2048)
        square = 0.0
        for q in quads:
            centred = j_ref[q] - average
            square = square + jnp.sum(centred * centred, axis=-1, keepdims=True)
        return average, lax.rsqrt(square * (1.0 / 2048) + EPSILON)

    average, merge_scale = joined_standard()
    for i, q in enumerate(quads):
        nj_ref[:, i * 512 : i * 512 + 512] = (
            (j_ref[q] - average) * merge_scale * gm[:, i * 512 : i * 512 + 512]
        ).astype(BF16)
    for i in range(6):
        cot_ref[i * 12 : i * 12 + 12] = coarse_cot[i].astype(F32)
    point("merge")

    def merge(i):
        cols = chunk(i, 256)
        weight = f_merge[:, :, :, :, cols].reshape(2048, 256)
        mg_ref[:, cols] = rounded(mm(nj_ref[...], weight))

    loop(4, merge)

    xhat, scale = standard(mg_ref[...])
    cn_ref[...] = (xhat * cg1[...]).astype(BF16)
    order = (gather.y, gather.dn, gather.up, gather.op)

    def coarse_attention(y):
        mixed = []
        packed = mm_t(cn_ref[...], f_triple[y].reshape(768, 1024))
        cqkv_ref[y] = packed
        for i in range(4):
            part = packed[:, i * 192 : i * 192 + 192].astype(BF16)
            p, turned, m = attend(part[:, :64], part[:, 64:128], part[:, 128:], None)
            cp_ref[y * 4 + i] = p
            cpt_ref[y * 4 + i] = turned
            mixed.append(m)
        cmix_ref[:, chunk(y, 256)] = jnp.concatenate(mixed, axis=-1).astype(BF16)

    for name, y in zip(("coarse", "coarse 1", "coarse 2", "coarse 3"), order):
        point(name)
        coarse_attention(y)
    point("coarse out")

    def coarse_project(i):
        cols = chunk(i, 256)
        weight = f_output[:, :, :, :, cols].reshape(1024, 256)
        cres_ref[:, cols] = mg_ref[:, cols] + mm(cmix_ref[...], weight)

    loop(4, coarse_project)
    xhat, scale = standard(cres_ref[...])
    cn_ref[...] = (xhat * cg2[...]).astype(BF16)
    hid_ref[...] = cres_ref[...]
    dn_ref[...] = jnp.zeros_like(dn_ref)

    def coarse_hidden(y):
        lower_weight = f_down[y].reshape(1024, 1024)
        grad = rounded(mm_t(cot_ref[...].astype(BF16), lower_weight))
        active = []
        total = dn_ref[...]
        for i in range(4):
            upper = f_up[y, i // 2, i % 2]
            value, slope = gelu_both(mm(cn_ref[...], upper))
            active.append(value.astype(BF16))
            total = total + mm_t((grad[:, i * 256 : i * 256 + 256] * slope).astype(BF16), upper)
        dn_ref[...] = total
        lifted_ref[y] = jnp.concatenate(active, axis=-1)

    for name, y in zip(("hidden", "hidden 1", "hidden 2", "hidden 3"), order):
        point(name)
        coarse_hidden(y)
    xhat, scale = standard(cres_ref[...])
    cres_ref[...] = cot_ref[...] + norm_pull(dn_ref[...], cg2[...], xhat, scale)

    def coarse_mix_pull(i):
        rows_of = f_output[i].reshape(256, 1024)
        cmix_ref[:, chunk(i, 256)] = mm_t(cres_ref[...].astype(BF16), rows_of).astype(BF16)

    loop(4, coarse_mix_pull)
    dn_ref[...] = jnp.zeros_like(dn_ref)

    def coarse_attention_pull(y):
        dmix = cmix_ref[:, chunk(y, 256)]
        packed = []
        for i in range(4):
            part = cqkv_ref[y, :, i * 192 : i * 192 + 192].astype(BF16)
            packed.extend(
                attend_pull(
                    part[:, :64], part[:, 64:128], part[:, 128:], cp_ref[y * 4 + i], cpt_ref[y * 4 + i],
                    dmix[:, i * 64 : i * 64 + 64],
                )
            )
        packed = jnp.concatenate(packed, axis=-1).astype(BF16)
        dn_ref[...] += mm(packed, f_triple[y].reshape(768, 1024))

    loop(4, coarse_attention_pull)
    xhat, scale = standard(mg_ref[...])
    cn_ref[...] = (cres_ref[...] + norm_pull(dn_ref[...], cg1[...], xhat, scale)).astype(BF16)

    def merge_pull(y):
        res_rows = chunk(y, WIN)
        grad_ref[res_rows] = rounded(mm_t(cn_ref[...], f_merge[y].reshape(512, 1024)))

    loop(4, merge_pull)
    first = 0.0
    second = 0.0
    for i, q in enumerate(quads):
        d = grad_ref[q] * gm[:, i * 512 : i * 512 + 512]
        first = first + jnp.sum(d, axis=-1, keepdims=True)
        second = second + jnp.sum(d * (j_ref[q] - average), axis=-1, keepdims=True)
    first = first * (1.0 / 2048)
    second = second * merge_scale * (1.0 / 2048)
    dqkv_ref[:, :512] = mm(m_tok_join[...], skip_cot[...])
    for i, q in enumerate(quads):
        d = grad_ref[q] * gm[:, i * 512 : i * 512 + 512]
        xhat = (j_ref[q] - average) * merge_scale
        grad_ref[q] = dqkv_ref[q, :512] + merge_scale * (d - first - xhat * second)

    win_ref[...] = grad_ref[...].astype(BF16)
    copies = exchange(2, mm(m_join_pack[...], win_ref[...]), ahead)
    grad_ref[...] = mm(m_join_own[...], win_ref[...])

    def coarse_lower(y):
        hid_ref[...] += mm(lifted_ref[y], f_down[y].reshape(1024, 1024))

    loop(4, coarse_lower)
    for i in range(6):
        coarse_out[i] = hid_ref[i * 12 : i * 12 + 12].astype(BF16)
    settle(copies)
    grad_ref[...] += mm(m_roll_got[...], halo_recv[2])

    def lower_pull(i):
        cols = chunk(i, 256)
        grad = rounded(mm_t(grad_ref[...].astype(BF16), wd[cols]))
        act_ref[:, cols] = (grad * slope_ref[:, cols].astype(F32)).astype(BF16)

    loop(8, lower_pull)

    def lift_pull(i):
        rows = chunk(i, 256)
        dres_ref[:, rows] = rounded(mm_t(act_ref[...], wu[rows]))

    loop(2, lift_pull)

    def second_pull(i):
        rows = chunk(i, 96)
        xhat, scale = standard(res_ref[rows])
        total = grad_ref[rows] + norm_pull(dres_ref[rows], g2[...], xhat, scale)
        dres_ref[rows] = total
        n_ref[rows] = total.astype(BF16)

    loop(3, second_pull)

    def out_pull(i):
        rows = chunk(i, 256)
        mix_ref[:, rows] = rounded(mm_t(n_ref[...], wo[rows]))

    loop(2, out_pull)

    def fine_attention_pull(w):
        rows = chunk(w, WIN)
        for pair in range(4):
            packed = []
            for h in (2 * pair, 2 * pair + 1):
                q, k, v = (
                    qkv_ref[rows, h * 192 + 64 * i : h * 192 + 64 * i + 64].astype(BF16) for i in range(3)
                )
                dm = mix_ref[rows, h * 64 : h * 64 + 64].astype(BF16)
                packed.extend(attend_pull(q, k, v, p_ref[w * 8 + h], pt_ref[w * 8 + h], dm))
            dqkv_ref[rows, pair * 384 : pair * 384 + 384] = jnp.concatenate(packed, axis=-1)

    loop(4, fine_attention_pull)

    def project_pull(i):
        rows = chunk(i, 256)
        grad_ref[:, rows] = rounded(mm_t(dqkv_ref[...].astype(BF16), wt[rows]))

    loop(2, project_pull)

    def first_pull(i):
        rows = chunk(i, 96)
        xhat, scale = standard(x_ref[rows])
        win_ref[rows] = (dres_ref[rows] + norm_pull(grad_ref[rows], g1[...], xhat, scale)).astype(BF16)

    loop(3, first_pull)
    copies = exchange(3, mm(m_back_pack[...], win_ref[...]), behind)
    grad_ref[...] = mm(m_back_own[...], win_ref[...])
    gather.finish()
    settle(copies)
    grad_out[...] = (grad_ref[...] + mm(m_back_got[...], halo_recv[3])).astype(BF16)


def place_results(*refs):
    for i in range(3):
        refs[3 + i][...] = refs[i][...]


def local(
    fine_tokens, region_labels, g1, wt, wo, g2, wu, wd, gm, s_merge, cg1, s_triple, s_output, cg2, s_up, s_down,
    skip_cot, coarse_cot,
):
    label_row = region_labels.reshape(1, TOKENS)
    moves = [jnp.asarray(m) for m in tables()]
    vmem = pl.BlockSpec(memory_space=pltpu.VMEM)
    held = pl.BlockSpec(memory_space=pl.ANY)
    s_triple = s_triple.T
    shards = (s_merge, s_triple, s_output, s_up, s_down)
    args = [
        fine_tokens.reshape(TOKENS, 512), label_row, g1[None], wt, wo, g2[None], wu, wd, gm[None], s_merge, cg1[None],
        s_triple, s_output, cg2[None], s_up, s_down, skip_cot.reshape(TOKENS, 512), coarse_cot, *moves,
    ]
    in_specs = [held if any(a is s for s in shards) else vmem for a in args]
    f32 = lambda *shape: pltpu.VMEM(shape, F32)
    bf16 = lambda *shape: pltpu.VMEM(shape, BF16)
    scratch = [bf16(4, 2, 2, *s.shape) for s in shards]
    scratch += [
        f32(288, 512), bf16(288, 512), f32(288, 8), f32(288, 1536), f32(32, 72, 72), f32(288, 512),
        f32(288, 512), bf16(288, 2048), bf16(288, 2048), bf16(288, 512),
        f32(288, 512), f32(288, 512), f32(288, 1536),
        f32(288, 512), bf16(72, 2048), f32(72, 1024), bf16(72, 1024), f32(4, 72, 768), f32(16, 72, 72),
        bf16(72, 1024), f32(72, 1024), f32(72, 1024), f32(72, 1024), f32(72, 1024),
        f32(32, 72, 72), f32(16, 72, 72), bf16(4, 72, 1024),
        bf16(4, HALO, 512), bf16(4, HALO, 512),
        pltpu.SemaphoreType.DMA((5,)), pltpu.SemaphoreType.DMA((5, SLOTS)), pltpu.SemaphoreType.DMA((5, SLOTS)),
        pltpu.SemaphoreType.DMA((4, 3)), pltpu.SemaphoreType.DMA((4, 3)),
    ]
    skip, coarse, grad = pl.pallas_call(
        kernel,
        out_shape=[
            jax.ShapeDtypeStruct((TOKENS, 512), BF16),
            jax.ShapeDtypeStruct((6, 12, 1024), BF16),
            jax.ShapeDtypeStruct((TOKENS, 512), BF16),
        ],
        in_specs=in_specs,
        out_specs=[vmem] * 3,
        scratch_shapes=scratch,
        compiler_params=pltpu.CompilerParams(
            collective_id=0, has_side_effects=True, vmem_limit_bytes=60 * 1024 * 1024
        ),
        name="backbone",
    )(*args)
    skip, coarse, grad = pl.pallas_call(
        place_results,
        out_shape=[jax.ShapeDtypeStruct(a.shape, a.dtype) for a in (skip, coarse, grad)],
        in_specs=[vmem] * 3,
        out_specs=[vmem] * 3,
        name="results",
    )(skip, coarse, grad)
    return skip.reshape(ROWS, COLS, 512), coarse, grad.reshape(ROWS, COLS, 512)


def solution(mesh):
    in_specs = (
        P("lat", "lon", None), P("lat", "lon"), P(), P(), P(), P(), P(), P(), P(), P("lon", None), P(),
        P(None, "lon"), P("lon", None), P(), P(None, "lon"), P("lon", None),
        P("lat", "lon", None), P("lat", "lon", None),
    )
    out_specs = (P("lat", "lon", None), P("lat", "lon", None), P("lat", "lon", None))
    return jax.shard_map(local, mesh=mesh, in_specs=in_specs, out_specs=out_specs, check_vma=False)
```
